512 devices in a mesh: row: 32 (over y, z_lo), col: 16 (over z_hi, x, core).
Axes of the slice: x: 4, y: 4, z: 16 (z_hi: 2, z_lo: 8; z = z_hi * 8 + z_lo), core: 2. Of those that a mesh axis runs over, the one named last changes fastest.
Arguments:
- picture_vectors: bfloat16 [20480, 1152], P(('row', 'col')), may hold values from -8 to 8
- caption_vectors: bfloat16 [20480, 1152], P(('col', 'row')), may hold values from -8 to 8
- scale_exponent: float32 [1], replicated, may hold values from 4 to 4.7
- score_shift: float32 [1], replicated, may hold values from -15 to -11
Outputs:
- image_grad: float32 [20480, 1152], P(('row', 'col'))
- text_grad: float32 [20480, 1152], P(('col', 'row'))
The draws below stay inside these ranges and needn't reach their ends.
All inputs are finite; a program needn't handle non-finite values.
Results may differ from the reference program's by a relative error of at most 0.029.
Values may be sent and summed in bfloat16 or wider, within the bound.
A program may use at most 64 MiB of HBM per device.

```python
import math
import jax
import jax.numpy as jnp
from jax import lax

D = 1152
SHARD = 40
BATCH = 20480
N_ROW = 32
N_COL = 16


def shared_parts(key):
    mean_key, pair_key = jax.random.split(key)
    mean_dir = jax.random.normal(mean_key, (1, D), jnp.float32)
    paired = jax.random.normal(pair_key, (BATCH, D), jnp.float32)
    return (mean_dir, paired)


def draw_picture_vectors(key, part):
    mean_dir, paired = shared_parts(key)
    key = jax.random.fold_in(key, 11)
    noise_key, scale_key = jax.random.split(key)
    noise = jax.random.normal(noise_key, (BATCH, D), jnp.float32)
    row_scale = jnp.exp(jax.random.uniform(scale_key, (BATCH, 1), jnp.float32, math.log(0.1), math.log(1.0)))
    mean_weight = 0.153
    pair_weight = 0.373
    values = row_scale * (mean_weight * mean_dir + pair_weight * paired + noise)
    return jnp.clip(values, -8.0, 8.0).astype(jnp.bfloat16)


def draw_caption_vectors(key, part):
    mean_dir, paired = shared_parts(key)
    key = jax.random.fold_in(key, 23)
    noise_key, scale_key = jax.random.split(key)
    noise = jax.random.normal(noise_key, (BATCH, D), jnp.float32)
    row_scale = jnp.exp(jax.random.uniform(scale_key, (BATCH, 1), jnp.float32, math.log(0.1), math.log(1.0)))
    mean_weight = 0.153
    pair_weight = 0.373
    values = row_scale * (mean_weight * mean_dir + pair_weight * paired + noise)
    return jnp.clip(values, -8.0, 8.0).astype(jnp.bfloat16)


def setup_inputs(seed: int = 0) -> dict:
    splits = jax.random.split(jax.random.key(seed), 5)
    picture_vectors = draw_picture_vectors(jax.random.fold_in(splits[4], 71), 0)
    caption_vectors = draw_caption_vectors(jax.random.fold_in(splits[4], 71), 0)
    scale_exponent = jnp.clip(jax.random.uniform(splits[2], (1,), jnp.float32, 4.0, 4.7), 4.0, 4.7)
    score_shift = jnp.clip(jax.random.uniform(splits[3], (1,), jnp.float32, -15.0, -11.0), -15.0, -11.0)
    return dict(picture_vectors=picture_vectors, caption_vectors=caption_vectors, scale_exponent=scale_exponent, score_shift=score_shift)


def unit_rows(values):
    values = values.astype(jnp.float32)
    inverse = lax.rsqrt(lax.optimization_barrier(jnp.sum(values * values, axis=1, keepdims=True)) + 1e-06)
    return (values * inverse, inverse)

def reference(picture_vectors, caption_vectors, scale_exponent, score_shift):
    smoothing_multiplier = jnp.exp(scale_exponent[0])
    block_offset = score_shift[0]
    image_unit, image_inverse = unit_rows(picture_vectors)
    text_unit, text_inverse = unit_rows(caption_vectors)
    image_half = image_unit.astype(jnp.bfloat16)
    text_halfway = text_unit.astype(jnp.bfloat16)
    block_rows = SHARD * N_COL
    group_rows = SHARD * N_ROW
    text_indices = jnp.arange(BATCH, dtype=jnp.int32)
    grouped_texts = text_halfway.reshape(N_COL, group_rows, D).astype(jnp.float32)

    def one_block(carry, index):
        start = (index * block_rows).astype(jnp.int32)
        image_batch = lax.dynamic_slice_in_dim(image_half, start, block_rows, 0)
        image_indices = start + jnp.arange(block_rows, dtype=jnp.int32)
        pair_logits = smoothing_multiplier * jnp.dot(image_batch, text_halfway.T, preferred_element_type=jnp.float32) + block_offset
        label_signs = jnp.where(image_indices[:, None] == text_indices[None, :], 1.0, -1.0).astype(jnp.float32)
        weight_values = (-label_signs * smoothing_multiplier * jax.nn.sigmoid(-label_signs * pair_logits)).astype(jnp.bfloat16)
        grouped = weight_values.reshape(block_rows, N_COL, group_rows).astype(jnp.float32)
        partial_value = jnp.einsum('rgt,gtd->grd', grouped, grouped_texts)
        image_dir = lax.optimization_barrier(jnp.sum(partial_value.astype(jnp.bfloat16).astype(jnp.float32), axis=0))
        text_part = jnp.dot(weight_values.T, image_batch, preferred_element_type=jnp.float32)
        carry = carry + text_part.astype(jnp.bfloat16).astype(jnp.float32)
        return (carry, image_dir)
    text_dir, image_dirs = lax.scan(one_block, jnp.zeros((BATCH, D), jnp.float32), jnp.arange(N_ROW, dtype=jnp.int32))
    image_dir = image_dirs.reshape(BATCH, D)
    image_grad = (image_dir - image_unit * lax.optimization_barrier(jnp.sum(image_unit * image_dir, axis=1, keepdims=True))) * image_inverse
    text_grad = (text_dir - text_unit * lax.optimization_barrier(jnp.sum(text_unit * text_dir, axis=1, keepdims=True))) * text_inverse
    return (image_grad, text_grad)
```

```python
import functools

import jax
import jax.numpy as jnp
from jax import lax
from jax.experimental import pallas as pl
from jax.experimental.pallas import tpu as pltpu
from jax.sharding import PartitionSpec as P

MESH = pl.DeviceIdType.MESH
D = 1152
SHARD = 40
UNIT = 80
CHUNK = 384
NCHUNK = 3
SLOTS = [
    (0, 0), (1, 0), (-1, 0), (2, 0), (0, 1), (0, -1), (1, 1), (1, -1),
    (-1, 1), (-1, -1), (2, 1), (2, -1), (0, 2), (1, 2), (-1, 2), (2, 2),
]
SLOT = {ab: i for i, ab in enumerate(SLOTS)}
RIGHT = (0, 2)
LEFT = (1, -1)
N_IMG = 16 * UNIT
N_TXT = 8 * UNIT
LINE = (0, 1, -1, 2)


def unit_rows(values):
    values = values.astype(jnp.float32)
    inverse = lax.rsqrt(jnp.sum(values * values, axis=1, keepdims=True) + 1e-06)
    return values * inverse, inverse


def cols(j):
    return pl.ds(j * CHUNK, CHUNK)


def kernel(
    pic, cap, scale, shift, gi, gt,
    rpic, rcap, oimg, img, txt, wt, pbuf, qbuf,
    psend, pd, rsb, rr, tf, tfr,
    rel_in, fin_in, half_in, afin_in, bsend, asend, last_send, last_in, sib_send, sib_in,
    ssem, rsem,
):
    r = lax.axis_index("row")
    q = lax.axis_index("col")
    x, y, z, c = (q % 8) // 2, r // 8, (q // 8) * 8 + r % 8, q % 2

    def dev(x, y, z, c):
        x, y, z = (x + 4) % 4, (y + 4) % 4, (z + 16) % 16
        return (y * 8 + z % 8, (z // 8) * 8 + x * 2 + c)

    sib = dev(x, y, z, 1 - c)
    sg = 1 - 2 * c

    def along_a(s):
        return dev(x + s * (1 - c), y + s * c, z, c)

    def along_b(s):
        return dev(x + s * c, y + s * (1 - c), z, c)

    ahead = dev(x, y, z + 2 * sg, c)
    behind = dev(x, y, z - 2 * sg, c)
    is0 = c == 0
    is1 = c == 1

    ids = {}
    started = []

    def rcopy(key, src, dst, to):
        i = ids.setdefault(key, len(ids))
        return pltpu.make_async_remote_copy(
            src_ref=src, dst_ref=dst, send_sem=ssem.at[i], recv_sem=rsem.at[i],
            device_id=to, device_id_type=MESH,
        )

    def send(key, src, dst, to, when=None):
        cp = rcopy(key, src, dst, to)
        if when is None:
            cp.start()
        else:
            pl.when(when)(cp.start)
        started.append((cp, when))

    def recv(key, dst, when=None):
        cp = rcopy(key, dst, dst, sib)
        if when is None:
            cp.wait_recv()
        else:
            pl.when(when)(cp.wait_recv)

    barrier = pltpu.get_barrier_semaphore()

    def greet(to):
        pl.semaphore_signal(barrier, inc=1, device_id=to, device_id_type=MESH)

    for to in (sib, along_a(1), along_a(-1), along_b(1), along_b(-1), ahead, behind, dev(x, y, z + 1, 1)):
        greet(to)

    @pl.when(is1)
    def _():
        greet(dev(x, y, z - 1, 1))
        greet(dev(x, y, z - 1, 0))
        pl.semaphore_wait(barrier, 10)

    @pl.when(is0)
    def _():
        pl.semaphore_wait(barrier, 8)

    send("rcap", cap, rcap, sib)
    send("rpic", pic, rpic, sib)
    own_txt = unit_rows(cap[...])[0]
    own_img = unit_rows(pic[...])[0]

    def both(mine, other):
        return jnp.concatenate(
            [jnp.where(is0, mine, other), jnp.where(is0, other, mine)], axis=0
        ).astype(jnp.bfloat16)

    recv("rcap", rcap)
    txt[0:UNIT] = both(own_txt, unit_rows(rcap[...])[0])

    def t_rows(slot):
        return pl.ds(pl.multiple_of(slot * UNIT, UNIT), UNIT)

    def fslot(k):
        return 2 * k - 1 + c

    def gslot(k):
        return 2 * k - c

    for j in range(NCHUNK):
        send(("t", 1, j), txt.at[0:UNIT, cols(j)], txt.at[t_rows(fslot(1)), cols(j)], ahead)
    recv("rpic", rpic)
    unit_img = both(own_img, unit_rows(rpic[...])[0])
    oimg[...] = unit_img

    def i_rows(slot):
        return pl.ds(slot * UNIT, UNIT)

    @pl.when(is0)
    def _():
        img[0:UNIT] = unit_img

    send("shift", oimg, img.at[0:UNIT], dev(x, y, z + 1, 1), when=is1)

    def isend(slot, to_slot, to):
        send(("i", to_slot), img.at[i_rows(slot)], img.at[i_rows(to_slot)], to)

    def irecv(slot):
        recv(("i", slot), img.at[i_rows(slot)])

    recv("shift", img.at[0:UNIT], when=is1)
    isend(0, SLOT[-1, 0], along_a(1))
    isend(0, SLOT[1, 0], along_a(-1))
    isend(0, SLOT[0, -1], along_b(1))
    isend(0, SLOT[0, 1], along_b(-1))

    D8 = pl.ds(7 * UNIT, UNIT)

    def d8_when(j):
        return is0 if j == 0 else is1

    def text_step(k):
        rows = t_rows(fslot(k))
        for j in range(NCHUNK):
            here = txt.at[rows, cols(j)]
            recv(("t", k, j), here)
            if k < 3:
                send(("t", k + 1, j), here, txt.at[t_rows(fslot(k + 1)), cols(j)], ahead)
            else:
                send(("t8", j), here, txt.at[D8, cols(j)], ahead, when=d8_when(j))
            send(("g", k, j), here, here, sib)

    def text_d8():
        for j in range(NCHUNK):
            here = txt.at[D8, cols(j)]
            recv(("t8", j), here, when=d8_when(j))
            send(("g8", j), here, here, sib, when=d8_when(j))

    def text_got(k):
        for j in range(NCHUNK):
            recv(("g", k, j), txt.at[t_rows(gslot(k)), cols(j)])

    def text_got8():
        for j in range(NCHUNK):
            recv(("g8", j), txt.at[D8, cols(j)], when=d8_when((j == 0) * 1))

    def line_step(a):
        slot = SLOT[a, 0]
        if a == 2:
            recv(("i3", 0), img.at[pl.ds(slot * UNIT, 48)])
            recv(("i3", 1), img.at[pl.ds(slot * UNIT + 48, 32)])
        else:
            irecv(slot)
        if a == -1:
            send(("i3", 0), img.at[pl.ds(slot * UNIT, 48)], img.at[pl.ds(3 * UNIT, 48)], along_a(1))
        if a == 1:
            send(("i3", 1), img.at[pl.ds(slot * UNIT + 48, 32)], img.at[pl.ds(3 * UNIT + 48, 32)], along_a(-1))
        isend(slot, SLOT[a, -1], along_b(1))
        isend(slot, SLOT[a, 1], along_b(-1))

    def side_step(a):
        irecv(SLOT[a, -1])
        if a in RIGHT:
            isend(SLOT[a, -1], SLOT[a, 2], along_b(1))
        irecv(SLOT[a, 1])
        if a in LEFT:
            isend(SLOT[a, 1], SLOT[a, 2], along_b(-1))

    lane = lax.broadcasted_iota(jnp.int32, (1, N_IMG), 1)
    zi = (z - c + 16) % 16
    img_ids = lane
    before = None
    for s, (a, b) in enumerate(SLOTS):
        xs = (x + a * (1 - c) + b * c + 4) % 4
        ys = (y + a * c + b * (1 - c) + 4) % 4
        base = ((ys * 8 + zi % 8) * 16 + (zi // 8) * 8 + xs * 2) * SHARD
        if s == 0:
            img_ids = img_ids + base
        else:
            img_ids = img_ids + jnp.where(lane >= s * UNIT, base - before - UNIT, 0)
        before = base

    row_in = lax.broadcasted_iota(jnp.int32, (UNIT, 1), 0)
    row_in = row_in + jnp.where(row_in >= SHARD, 32 * SHARD - SHARD, 0)

    def txt_ids(slot):
        step = 0 if slot == 0 else (8 if slot == 7 else (-2 * ((slot + 1) // 2) if slot % 2 else slot))
        zt = (z + step + 16) % 16
        return row_in + (((zt // 8) * 8 + x * 2) * 32 + y * 8 + zt % 8) * SHARD

    smooth = jnp.exp(jnp.full((1, 128), scale[0], jnp.float32))[:, :1]
    offset = shift[0]

    def weights(t0, t1, i0, i1):
        dots = lax.dot_general(
            txt[t0:t1], img[i0:i1], (((1,), (1,)), ((), ())), preferred_element_type=jnp.float32
        )
        logits = smooth * dots + offset
        tid = jnp.concatenate([txt_ids(s) for s in range(t0 // UNIT, t1 // UNIT)], axis=0)
        match = tid == img_ids[:, i0:i1]
        value = smooth / (1.0 + jnp.exp(jnp.where(match, logits, -logits)))
        wt[t0:t1, i0:i1] = jnp.where(match, -value, value).astype(jnp.bfloat16)

    line_step(-1)
    line_step(1)
    text_step(1)
    side_step(0)
    line_step(2)
    text_got(1)
    text_step(2)
    side_step(1)
    weights(0, 240, 0, 640)
    side_step(-1)
    text_got(2)
    weights(240, 400, 0, 640)
    text_step(3)
    side_step(2)
    irecv(SLOT[0, 2])
    irecv(SLOT[1, 2])
    irecv(SLOT[-1, 2])
    text_d8()
    irecv(SLOT[2, 2])
    weights(0, 240, 640, 1280)
    weights(240, 400, 640, 1280)
    text_got(3)
    text_got8()
    weights(400, 640, 0, 640)
    weights(400, 640, 640, 1280)

    def text_part(t0, t1):
        pbuf[t0:t1] = jnp.dot(wt[t0:t1], img[...], preferred_element_type=jnp.float32)

    def image_part(i0, i1):
        qbuf[i0:i1] = lax.dot_general(
            wt[:, i0:i1], txt[...], (((0,), (0,)), ((), ())), preferred_element_type=jnp.float32
        )

    def part_out(k):
        psend[k] = pbuf[t_rows(gslot(k))].astype(jnp.bfloat16)
        for j in range(NCHUNK):
            send(("p", k, j), psend.at[k, :, cols(j)], pd.at[k, :, cols(j)], sib)

    def part_out8():
        psend[0] = pbuf[D8].astype(jnp.bfloat16)
        for j in range(NCHUNK):
            send(("p", 0, j), psend.at[0, :, cols(j)], pd.at[0, :, cols(j)], sib, when=d8_when((j == 0) * 1))

    def back8():
        for j in range(NCHUNK):
            @pl.when(d8_when(j))
            def _(j=j):
                recv(("p", 0, j), pd.at[0, :, cols(j)])
                total = pbuf[D8, cols(j)] + pd[0, :, cols(j)].astype(jnp.float32)
                rsb[0, :, cols(j)] = total.astype(jnp.bfloat16)
            send(("b", 0, j), rsb.at[0, :, cols(j)], rr.at[3, :, cols(j)], behind, when=d8_when(j))

    def back_chunk(k, j):
        recv(("p", k, j), pd.at[k, :, cols(j)])
        total = pbuf[t_rows(fslot(k)), cols(j)] + pd[k, :, cols(j)].astype(jnp.float32)
        if k < 3:
            recv(("b", k + 1, j), rr.at[k, :, cols(j)])
            rsb[k, :, cols(j)] = (total + rr[k, :, cols(j)].astype(jnp.float32)).astype(jnp.bfloat16)
        else:
            mine = d8_when(j)

            @pl.when(mine)
            def _():
                recv(("b", 0, j), rr.at[3, :, cols(j)])
                rsb[k, :, cols(j)] = (total + rr[3, :, cols(j)].astype(jnp.float32)).astype(jnp.bfloat16)

            @pl.when(jnp.logical_not(mine))
            def _():
                rsb[k, :, cols(j)] = total.astype(jnp.bfloat16)
        send(("b", k, j), rsb.at[k, :, cols(j)], rr.at[k - 1, :, cols(j)], behind)

    def back(k):
        for j in range(NCHUNK):
            back_chunk(k, j)

    def q_unit(slot):
        return qbuf[slot * UNIT:(slot + 1) * UNIT]

    def opposite(n):
        a = LINE[n]
        bsend[n] = q_unit(SLOT[a, 2]).astype(jnp.bfloat16)
        send(("ro", a), bsend.at[n], rel_in.at[n], along_b(1 if a in RIGHT else -1))

    def toward(n, s):
        a = LINE[n]
        m = 4 + n if s == 1 else 8 + n
        total = q_unit(SLOT[a, s])
        if (a in RIGHT) == (s == 1):
            recv(("ro", a), rel_in.at[n])
            total = total + rel_in[n].astype(jnp.float32)
        bsend[m] = total.astype(jnp.bfloat16)
        send(("rf", a, s), bsend.at[m], fin_in.at[m - 4], along_b(s))

    def line_total(n):
        a = LINE[n]
        recv(("rf", a, 1), fin_in.at[n])
        recv(("rf", a, -1), fin_in.at[4 + n])
        return (
            q_unit(SLOT[a, 0]) + fin_in[n].astype(jnp.float32) + fin_in[4 + n].astype(jnp.float32)
        )

    text_part(400, 640)
    part_out8()
    part_out(3)
    image_part(896, 1280)
    for n in range(4):
        opposite(n)
    back8()
    for j in range(NCHUNK):
        @pl.when(jnp.logical_not(d8_when(j)))
        def _(j=j):
            recv(("p", 3, j), pd.at[3, :, cols(j)])
            total = pbuf[t_rows(fslot(3)), cols(j)] + pd[3, :, cols(j)].astype(jnp.float32)
            rsb[3, :, cols(j)] = total.astype(jnp.bfloat16)
        send(("b", 3, j), rsb.at[3, :, cols(j)], rr.at[2, :, cols(j)], behind, when=jnp.logical_not(d8_when(j)))
    image_part(256, 896)
    for n in range(4):
        for s in (1, -1):
            if (LINE[n] in RIGHT) != (s == 1):
                toward(n, s)
    for j in range(NCHUNK):
        @pl.when(d8_when(j))
        def _(j=j):
            recv(("p", 3, j), pd.at[3, :, cols(j)])
            recv(("b", 0, j), rr.at[3, :, cols(j)])
            total = pbuf[t_rows(fslot(3)), cols(j)] + pd[3, :, cols(j)].astype(jnp.float32)
            rsb[3, :, cols(j)] = (total + rr[3, :, cols(j)].astype(jnp.float32)).astype(jnp.bfloat16)
        send(("b", 3, j), rsb.at[3, :, cols(j)], rr.at[2, :, cols(j)], behind, when=d8_when(j))
    text_part(240, 400)
    part_out(2)
    for n in range(4):
        for s in (1, -1):
            if (LINE[n] in RIGHT) == (s == 1):
                toward(n, s)
    text_part(0, 240)
    part_out(1)
    back(2)
    image_part(0, 256)
    opp = line_total(3)
    asend[0] = opp.astype(jnp.bfloat16)
    send(("ra", 0), asend.at[0, pl.ds(0, 48)], half_in.at[pl.ds(0, 48)], along_a(1))
    send(("ra", 1), asend.at[0, pl.ds(48, 32)], half_in.at[pl.ds(48, 32)], along_a(-1))
    back(1)
    plus = line_total(1)
    recv(("ra", 0), half_in.at[pl.ds(0, 48)])
    asend[1] = jnp.concatenate(
        [plus[:48] + half_in[0:48].astype(jnp.float32), plus[48:]], axis=0
    ).astype(jnp.bfloat16)
    send(("rb", 0), asend.at[1], afin_in.at[0], along_a(1))
    minus = line_total(2)
    recv(("ra", 1), half_in.at[pl.ds(48, 32)])
    asend[2] = jnp.concatenate(
        [minus[:48], minus[48:] + half_in[48:80].astype(jnp.float32)], axis=0
    ).astype(jnp.bfloat16)
    send(("rb", 1), asend.at[2], afin_in.at[1], along_a(-1))

    for j in range(NCHUNK):
        recv(("b", 1, j), rr.at[0, :, cols(j)])
    tf[...] = pbuf[0:UNIT] + rr[0].astype(jnp.float32)

    def half(core):
        return pl.ds(pl.multiple_of(core * SHARD, SHARD), SHARD)

    send("tf", tf.at[half(1 - c)], tfr, sib)

    own = line_total(0)
    recv(("rb", 0), afin_in.at[0])
    recv(("rb", 1), afin_in.at[1])
    own = own + afin_in[0].astype(jnp.float32) + afin_in[1].astype(jnp.float32)

    @pl.when(is1)
    def _():
        for h in range(2):
            last_send[h, 0:SHARD] = own[h * SHARD:(h + 1) * SHARD].astype(jnp.bfloat16)
            last_send[h, SHARD:48] = jnp.zeros((48 - SHARD, D), jnp.bfloat16)

    @pl.when(is0)
    def _():
        sib_send[...] = own

    send(("last", 0), last_send.at[0], last_in, dev(x, y, z - 1, 0), when=is1)
    send(("last", 1), last_send.at[1], last_in, dev(x, y, z - 1, 1), when=is1)
    send("sib", sib_send.at[pl.ds(SHARD, SHARD)], sib_in, sib, when=is0)

    recv("tf", tfr)
    v, v_inv = unit_rows(cap[...])
    text_dir = tf[half(c)] + tfr[...]
    gt[...] = (text_dir - v * jnp.sum(v * text_dir, axis=1, keepdims=True)) * v_inv

    recv("sib", sib_in, when=is1)
    recv(("last", 0), last_in, when=is0)
    recv(("last", 1), last_in, when=is1)

    @pl.when(is0)
    def _():
        sib_in[...] = sib_send[0:SHARD]

    u, u_inv = unit_rows(pic[...])
    image_dir = sib_in[...] + last_in[0:SHARD].astype(jnp.float32)
    gi[...] = (image_dir - u * jnp.sum(u * image_dir, axis=1, keepdims=True)) * u_inv

    for cp, when in started:
        if when is None:
            cp.wait_send()
        else:
            pl.when(when)(cp.wait_send)


def body(picture_vectors, caption_vectors, scale_exponent, score_shift):
    bf16, f32 = jnp.bfloat16, jnp.float32
    vmem = pl.BlockSpec(memory_space=pltpu.VMEM)
    smem = pl.BlockSpec(memory_space=pltpu.SMEM)
    out = jax.ShapeDtypeStruct((SHARD, D), f32)
    return pl.pallas_call(
        kernel,
        out_shape=(out, out),
        in_specs=[vmem, vmem, smem, smem],
        out_specs=(vmem, vmem),
        scratch_shapes=[
            pltpu.VMEM((SHARD, D), bf16),
            pltpu.VMEM((SHARD, D), bf16),
            pltpu.VMEM((UNIT, D), bf16),
            pltpu.VMEM((N_IMG, D), bf16),
            pltpu.VMEM((N_TXT, D), bf16),
            pltpu.VMEM((N_TXT, N_IMG), bf16),
            pltpu.VMEM((N_TXT, D), f32),
            pltpu.VMEM((N_IMG, D), f32),
            pltpu.VMEM((4, UNIT, D), bf16),
            pltpu.VMEM((4, UNIT, D), bf16),
            pltpu.VMEM((4, UNIT, D), bf16),
            pltpu.VMEM((4, UNIT, D), bf16),
            pltpu.VMEM((UNIT, D), f32),
            pltpu.VMEM((SHARD, D), f32),
            pltpu.VMEM((4, UNIT, D), bf16),
            pltpu.VMEM((8, UNIT, D), bf16),
            pltpu.VMEM((UNIT, D), bf16),
            pltpu.VMEM((2, UNIT, D), bf16),
            pltpu.VMEM((12, UNIT, D), bf16),
            pltpu.VMEM((3, UNIT, D), bf16),
            pltpu.VMEM((2, 48, D), bf16),
            pltpu.VMEM((48, D), bf16),
            pltpu.VMEM((UNIT, D), f32),
            pltpu.VMEM((SHARD, D), f32),
            pltpu.SemaphoreType.DMA((128,)),
            pltpu.SemaphoreType.DMA((128,)),
        ],
        compiler_params=pltpu.CompilerParams(
            collective_id=0, has_side_effects=True, vmem_limit_bytes=56 * 2**20
        ),
    )(picture_vectors, caption_vectors, scale_exponent, score_shift)


def solution(mesh):
    return jax.shard_map(
        body,
        mesh=mesh,
        in_specs=(P(("row", "col"), None), P(("col", "row"), None), P(), P()),
        out_specs=(P(("row", "col"), None), P(("col", "row"), None)),
        check_vma=False,
    )
```

```python
import jax
import jax.numpy as jnp
from jax import lax
from jax.experimental import pallas as pl
from jax.experimental.pallas import tpu as pltpu
from jax.sharding import PartitionSpec as P

MESH = pl.DeviceIdType.MESH
D = 1152
SHARD = 40
UNIT = 80
SLOTS = (
    (0, 0), (1, 0), (-1, 0), (2, 0), (0, 1), (0, -1), (1, 1), (1, -1),
    (-1, 1), (-1, -1), (2, 1), (2, -1), (0, 2), (1, 2), (-1, 2), (2, 2),
)
SLOT = {ab: i for i, ab in enumerate(SLOTS)}
RIGHT = (0, 2)
LINE = (0, 1, -1, 2)
N_IMG = 16 * UNIT
N_TXT = 8 * UNIT
T_ROWS = ((0, 32), (32, 32), (64, 16))
I_ROWS = ((0, 48), (48, 32))
FAR = ((0,), (1, 2))
T_GROUPS = ((0, 240), (240, 400), (400, 560), (560, 640))
I_GROUPS = ((0, 640), (640, 1024), (1024, 1280))
Q_GROUPS = ((896, 1280), (256, 896), (0, 256))
ORDER = (
    (
        ('t', 0, 0), ('t', 0, 1), ('t', 0, 2), ('i', 0, 0), ('i', 0, 1), ('i', 1, 0), ('i', 2, 0), ('i', 4, 0),
        ('i', 5, 0), ('t', 1, 0), ('i', 1, 1), ('i', 2, 1), ('i', 4, 1), ('i', 5, 1), ('t', 1, 1), ('t', 1, 2),
        ('i', 3, 1), ('t', 2, 0), ('i', 3, 0), ('i', 6, 0), ('i', 7, 0), ('i', 8, 0), ('i', 9, 0), ('t', 2, 1),
        ('i', 6, 1), ('t', 2, 2), ('i', 12, 0), ('i', 8, 1), ('i', 7, 1), ('W', 0, 0), ('t', 3, 0), ('i', 9, 1),
        ('W', 1, 0), ('i', 10, 1), ('i', 12, 1), ('t', 3, 1), ('i', 10, 0), ('t', 3, 2), ('i', 11, 1), ('i', 13, 0),
        ('W', 2, 0), ('i', 11, 0), ('i', 14, 0), ('t', 4, 0), ('W', 0, 1), ('W', 1, 1), ('i', 13, 1), ('W', 2, 1),
        ('i', 14, 1), ('i', 15, 1), ('W', 3, 0), ('W', 3, 1), ('i', 15, 0), ('W', 0, 2), ('W', 1, 2), ('W', 2, 2),
        ('W', 3, 2), ('P', 2), ('pp', 3), ('P', 3), ('pp', 0), ('Q', 0), ('ro', 0, 0), ('ro', 0, 1), ('ro', 1, 0),
        ('ro', 1, 1), ('ro', -1, 0), ('ro', -1, 1), ('ro', 2, 0), ('ro', 2, 1), ('Q', 1), ('rf', 0, -1, 0),
        ('rf', 0, -1, 1), ('rf', 1, 1, 0), ('rf', 1, 1, 1), ('rf', -1, 1, 0), ('rf', -1, 1, 1), ('rf', 2, -1, 0),
        ('rf', 2, -1, 1), ('b', 3, 1), ('b', 3, 2), ('b', 0, 0), ('rf', 0, 1, 0), ('rf', 1, -1, 0), ('rf', 0, 1, 1),
        ('P', 1), ('pp', 2), ('rf', 1, -1, 1), ('rf', 2, 1, 0), ('rf', -1, -1, 0), ('Q', 2), ('rf', 2, 1, 1),
        ('rf', -1, -1, 1), ('P', 0), ('pp', 1), ('b', 2, 1), ('b', 2, 2), ('b', 3, 0), ('b', 1, 1), ('la', 1, 1),
        ('b', 1, 2), ('la', 2, 0), ('la', -1, 0), ('la', 2, 1), ('b', 2, 0), ('la', 1, 0), ('la', -1, 1),
        ('b', 1, 0), ('own',), ('tf',), ('gt',), ('gi',),
    ),
    (
        ('t', 0, 0), ('t', 0, 1), ('t', 0, 2), ('i', 0, 0), ('i', 0, 1), ('t', 1, 0), ('t', 1, 1), ('t', 1, 2),
        ('i', 1, 0), ('i', 2, 0), ('i', 4, 0), ('i', 5, 0), ('i', 1, 1), ('i', 2, 1), ('i', 4, 1), ('i', 5, 1),
        ('t', 2, 0), ('t', 2, 1), ('t', 2, 2), ('i', 6, 0), ('i', 7, 0), ('i', 8, 0), ('i', 9, 0), ('t', 3, 0),
        ('i', 3, 1), ('i', 6, 1), ('i', 12, 0), ('i', 8, 1), ('i', 7, 1), ('t', 3, 1), ('i', 9, 1), ('i', 13, 0),
        ('t', 3, 2), ('i', 3, 0), ('W', 0, 0), ('i', 12, 1), ('i', 14, 0), ('W', 1, 0), ('i', 11, 1), ('i', 10, 1),
        ('W', 2, 0), ('i', 13, 1), ('t', 4, 1), ('i', 14, 1), ('i', 11, 0), ('t', 4, 2), ('W', 3, 0), ('Q', 2),
        ('i', 10, 0), ('i', 15, 1), ('W', 0, 1), ('W', 1, 1), ('W', 2, 1), ('W', 3, 1), ('Q', 1), ('i', 15, 0),
        ('rf', 0, -1, 0), ('rf', 0, -1, 1), ('rf', 1, 1, 0), ('rf', 1, 1, 1), ('rf', -1, 1, 0), ('rf', -1, 1, 1),
        ('W', 0, 2), ('W', 1, 2), ('W', 2, 2), ('W', 3, 2), ('P', 2), ('pp', 3), ('b', 3, 0), ('P', 3), ('pp', 0),
        ('b', 0, 1), ('b', 0, 2), ('Q', 0), ('ro', 0, 0), ('ro', 0, 1), ('ro', 1, 0), ('ro', 1, 1), ('ro', -1, 0),
        ('ro', -1, 1), ('ro', 2, 0), ('rf', 2, -1, 0), ('ro', 2, 1), ('rf', 2, -1, 1), ('P', 1), ('pp', 2), ('P', 0),
        ('pp', 1), ('b', 2, 0), ('rf', 0, 1, 0), ('b', 3, 1), ('rf', 1, -1, 0), ('rf', 0, 1, 1), ('b', 3, 2),
        ('rf', 1, -1, 1), ('rf', 2, 1, 0), ('rf', -1, -1, 0), ('rf', 2, 1, 1), ('rf', -1, -1, 1), ('b', 1, 0),
        ('b', 2, 1), ('la', 2, 0), ('b', 2, 2), ('la', 2, 1), ('la', 1, 1), ('la', -1, 0), ('la', 1, 0), ('b', 1, 1),
        ('la', -1, 1), ('b', 1, 2), ('own',), ('tf',), ('gt',), ('gi',),
    ),
)


def unit_rows(values):
    values = values.astype(jnp.float32)
    inverse = lax.rsqrt(jnp.sum(values * values, axis=1, keepdims=True) + 1e-06)
    return values * inverse, inverse


def kernel(
    pic, cap, scale, shift, gi, gt,
    raw_cap, raw_a, raw_b, img, txt, wt, pbuf, qbuf,
    psend, pd, rsb, rr, tf, tfr,
    rel_in, fin_in, half_in, afin_in, bsend, asend, last_send, last_in, sib_send, sib_in,
    ssem, rsem,
):
    r = lax.axis_index("row")
    q = lax.axis_index("col")
    x, y, z, core = (q % 8) // 2, r // 8, (q // 8) * 8 + r % 8, q % 2

    def dev(x, y, z, c):
        x, y, z = (x + 4) % 4, (y + 4) % 4, (z + 16) % 16
        return (y * 8 + z % 8, (z // 8) * 8 + x * 2 + c)

    barrier = pltpu.get_barrier_semaphore()

    def greet(to):
        pl.semaphore_signal(barrier, inc=1, device_id=to, device_id_type=MESH)

    for to in (
        dev(x, y, z, 1 - core), dev(x + 1, y, z, core), dev(x - 1, y, z, core), dev(x, y + 1, z, core),
        dev(x, y - 1, z, core), dev(x, y, z + 2, core), dev(x, y, z - 2, core), dev(x, y, z + 1, 1),
    ):
        greet(to)

    @pl.when(core == 1)
    def _():
        greet(dev(x, y, z - 1, 1))
        greet(dev(x, y, z - 1, 0))

    ids = {}
    offset = shift[0]

    def one_core(c):
        sib = dev(x, y, z, 1 - c)
        sg = 1 - 2 * c
        ahead = dev(x, y, z + 2 * sg, c)
        behind = dev(x, y, z - 2 * sg, c)
        started = []

        def along_a(s):
            return dev(x + s * (1 - c), y + s * c, z, c)

        def along_b(s):
            return dev(x + s * c, y + s * (1 - c), z, c)

        def rcopy(key, src, dst, to):
            i = ids.setdefault(key, len(ids))
            return pltpu.make_async_remote_copy(
                src_ref=src, dst_ref=dst, send_sem=ssem.at[i], recv_sem=rsem.at[i],
                device_id=to, device_id_type=MESH,
            )

        def send(key, src, dst, to):
            cp = rcopy(key, src, dst, to)
            cp.start()
            started.append(cp)

        def recv(key, dst):
            rcopy(key, dst, dst, sib).wait_recv()

        smooth = jnp.exp(jnp.full((1, 128), scale[0], jnp.float32))[:, :1]
        lane = lax.broadcasted_iota(jnp.int32, (1, N_IMG), 1)
        zi = (z - c + 16) % 16
        img_ids = lane
        before = None
        for s, (a, b) in enumerate(SLOTS):
            xs = (x + a * (1 - c) + b * c + 4) % 4
            ys = (y + a * c + b * (1 - c) + 4) % 4
            base = ((ys * 8 + zi % 8) * 16 + (zi // 8) * 8 + xs * 2) * SHARD
            if s == 0:
                img_ids = img_ids + base
            else:
                img_ids = img_ids + jnp.where(lane >= s * UNIT, base - before - UNIT, 0)
            before = base
        row_in = lax.broadcasted_iota(jnp.int32, (UNIT, 1), 0)
        row_in = row_in + jnp.where(row_in >= SHARD, 32 * SHARD - SHARD, 0)

        def txt_ids(slot):
            step = 0 if slot == 0 else (8 if slot == 7 else (-2 * ((slot + 1) // 2) if slot % 2 else slot))
            zt = (z + step + 16) % 16
            return row_in + (((zt // 8) * 8 + x * 2) * 32 + y * 8 + zt % 8) * SHARD

        own_txt = unit_rows(cap[...])[0]
        if c == 0:
            own_img = unit_rows(pic[...])[0]
        pl.semaphore_wait(barrier, 10 if c else 8)
        send("cap", cap, raw_cap, sib)
        if c == 0:
            send("pic_a", pic, raw_a, dev(x, y, z + 1, 1))
        else:
            send("pic_0", pic, raw_a, sib)
            send("pic_b", pic, raw_b, dev(x, y, z + 1, 1))

        def both(one, two):
            return jnp.concatenate([one, two], axis=0).astype(jnp.bfloat16)

        def f_slot(k):
            return 0 if k == 0 else (7 if k == 4 else 2 * k - 1 + c)

        def g_slot(k):
            return 7 if k == 4 else 2 * k - c

        def t_piece(slot, h):
            return pl.ds(slot * UNIT + T_ROWS[h][0], T_ROWS[h][1])

        def i_piece(slot, h):
            return pl.ds(slot * UNIT + I_ROWS[h][0], I_ROWS[h][1])

        got = set()

        def need(key, dst):
            if key not in got:
                got.add(key)
                recv(key, dst)

        def step_t(k, h):
            if k == 0:
                if h == 0:
                    recv("cap", raw_cap)
                    other = unit_rows(raw_cap[...])[0]
                    txt[0:UNIT] = both(own_txt, other) if c == 0 else both(other, own_txt)
            else:
                need(("t", k, h), txt.at[t_piece(f_slot(k), h)])
            here = txt.at[t_piece(f_slot(k), h)]
            if k < 3 or (k == 3 and h in FAR[c]):
                send(("t", k + 1, h), here, txt.at[t_piece(f_slot(k + 1), h)], ahead)
            if k > 0:
                send(("g", k, h), here, here, sib)

        def step_i(s, h):
            a, b = SLOTS[s]

            def forward(to_slot, to):
                send(("i", to_slot, h), img.at[i_piece(s, h)], img.at[i_piece(to_slot, h)], to)

            if s == 0:
                if h == 0:
                    if c == 0:
                        recv("pic_0", raw_a)
                        img[0:UNIT] = both(own_img, unit_rows(raw_a[...])[0])
                    else:
                        recv("pic_a", raw_a)
                        recv("pic_b", raw_b)
                        img[0:UNIT] = both(unit_rows(raw_a[...])[0], unit_rows(raw_b[...])[0])
                forward(SLOT[-1, 0], along_a(1))
                forward(SLOT[1, 0], along_a(-1))
            else:
                need(("i", s, h), img.at[i_piece(s, h)])
            if b == 0:
                if a == -1 and h == 0:
                    forward(SLOT[2, 0], along_a(1))
                if a == 1 and h == 1:
                    forward(SLOT[2, 0], along_a(-1))
                forward(SLOT[a, -1], along_b(1))
                forward(SLOT[a, 1], along_b(-1))
            if b == -1 and a in RIGHT:
                forward(SLOT[a, 2], along_b(1))
            if b == 1 and a not in RIGHT:
                forward(SLOT[a, 2], along_b(-1))

        def text_needs(slot):
            if slot == 0:
                return
            k = 4 if slot == 7 else (slot + 1) // 2
            for h in range(len(T_ROWS)):
                mine = h in FAR[c] if k == 4 else (slot % 2 == 1) == (c == 0)
                if not mine:
                    need(("g", k, h), txt.at[t_piece(slot, h)])

        def step_w(gt_, gi_):
            t0, t1 = T_GROUPS[gt_]
            i0, i1 = I_GROUPS[gi_]
            for s in range(t0 // UNIT, t1 // UNIT):
                text_needs(s)
            dots = lax.dot_general(
                txt[t0:t1], img[i0:i1], (((1,), (1,)), ((), ())), preferred_element_type=jnp.float32
            )
            logits = smooth * dots + offset
            tid = jnp.concatenate([txt_ids(s) for s in range(t0 // UNIT, t1 // UNIT)], axis=0)
            match = tid == img_ids[:, i0:i1]
            value = smooth / (1.0 + jnp.exp(jnp.where(match, logits, -logits)))
            wt[t0:t1, i0:i1] = jnp.where(match, -value, value).astype(jnp.bfloat16)

        def step_p(g):
            t0, t1 = T_GROUPS[g]
            pbuf[t0:t1] = jnp.dot(wt[t0:t1], img[...], preferred_element_type=jnp.float32)

        def step_q(g):
            i0, i1 = Q_GROUPS[g]
            qbuf[i0:i1] = lax.dot_general(
                wt[:, i0:i1], txt[...], (((0,), (0,)), ((), ())), preferred_element_type=jnp.float32
            )

        def step_pp(k):
            slot = g_slot(k) if k else 7
            psend[k] = pbuf[slot * UNIT:(slot + 1) * UNIT].astype(jnp.bfloat16)
            for h, (o, n) in enumerate(T_ROWS):
                if k > 0 or h in FAR[1 - c]:
                    send(("p", k, h), psend.at[k, pl.ds(o, n)], pd.at[k, pl.ds(o, n)], sib)

        def step_b(k, h):
            o, n = T_ROWS[h]
            slot = f_slot(k) if k else 7
            recv(("p", k, h), pd.at[k, pl.ds(o, n)])
            total = pbuf[slot * UNIT + o:slot * UNIT + o + n] + pd[k, o:o + n].astype(jnp.float32)
            more = {3: 0, 2: 3, 1: 2}.get(k)
            if k in (1, 2) or (k == 3 and h in FAR[c]):
                recv(("b", more, h), rr.at[k, pl.ds(o, n)])
                total = total + rr[k, o:o + n].astype(jnp.float32)
            rsb[k, o:o + n] = total.astype(jnp.bfloat16)
            to = 3 if k == 0 else k - 1
            send(("b", k, h), rsb.at[k, pl.ds(o, n)], rr.at[to, pl.ds(o, n)], behind)

        def step_tf():
            for h, (o, n) in enumerate(T_ROWS):
                recv(("b", 1, h), rr.at[0, pl.ds(o, n)])
            tf[...] = pbuf[0:UNIT] + rr[0].astype(jnp.float32)
            send("tf", tf.at[pl.ds((1 - c) * SHARD, SHARD)], tfr, sib)

        def step_gt():
            recv("tf", tfr)
            v, v_inv = unit_rows(cap[...])
            text_dir = tf[c * SHARD:(c + 1) * SHARD] + tfr[...]
            gt[...] = (text_dir - v * jnp.sum(v * text_dir, axis=1, keepdims=True)) * v_inv

        def q_piece(slot, h):
            o, n = I_ROWS[h]
            return qbuf[slot * UNIT + o:slot * UNIT + o + n]

        def step_ro(a, h):
            n = LINE.index(a)
            o, m = I_ROWS[h]
            bsend[n, o:o + m] = q_piece(SLOT[a, 2], h).astype(jnp.bfloat16)
            here = pl.ds(o, m)
            send(("ro", a, h), bsend.at[n, here], rel_in.at[n, here], along_b(1 if a in RIGHT else -1))

        def step_rf(a, s, h):
            n = LINE.index(a)
            o, m = I_ROWS[h]
            here = pl.ds(o, m)
            total = q_piece(SLOT[a, s], h)
            if (a in RIGHT) == (s == 1):
                recv(("ro", a, h), rel_in.at[n, here])
                total = total + rel_in[n, o:o + m].astype(jnp.float32)
            to = n if s == 1 else 4 + n
            bsend[4 + to, o:o + m] = total.astype(jnp.bfloat16)
            send(("rf", a, s, h), bsend.at[4 + to, here], fin_in.at[to, here], along_b(s))

        def line_total(a, h):
            n = LINE.index(a)
            o, m = I_ROWS[h]
            here = pl.ds(o, m)
            recv(("rf", a, 1, h), fin_in.at[n, here])
            recv(("rf", a, -1, h), fin_in.at[4 + n, here])
            return (
                q_piece(SLOT[a, 0], h)
                + fin_in[n, o:o + m].astype(jnp.float32)
                + fin_in[4 + n, o:o + m].astype(jnp.float32)
            )

        def step_la(a, h):
            o, m = I_ROWS[h]
            here = pl.ds(o, m)
            total = line_total(a, h)
            i = {2: 0, 1: 1, -1: 2}[a]
            if (a, h) in ((1, 0), (-1, 1)):
                recv(("ra", h), half_in.at[here])
                total = total + half_in[o:o + m].astype(jnp.float32)
            asend[i, o:o + m] = total.astype(jnp.bfloat16)
            if a == 2:
                send(("ra", h), asend.at[i, here], half_in.at[here], along_a(1 if h == 0 else -1))
            else:
                send(("rb", a, h), asend.at[i, here], afin_in.at[i - 1, here], along_a(a))

        def step_own():
            parts = []
            for h, (o, m) in enumerate(I_ROWS):
                total = line_total(0, h)
                for i, a in enumerate((1, -1)):
                    recv(("rb", a, h), afin_in.at[i, pl.ds(o, m)])
                    total = total + afin_in[i, o:o + m].astype(jnp.float32)
                parts.append(total)
            own = jnp.concatenate(parts, axis=0)
            if c == 0:
                sib_send[...] = own
                send("sib", sib_send.at[pl.ds(SHARD, SHARD)], sib_in, sib)
            else:
                for h in range(2):
                    last_send[h, 0:SHARD] = own[h * SHARD:(h + 1) * SHARD].astype(jnp.bfloat16)
                    last_send[h, SHARD:48] = jnp.zeros((48 - SHARD, D), jnp.bfloat16)
                send(("last", 0), last_send.at[0], last_in, dev(x, y, z - 1, 0))
                send(("last", 1), last_send.at[1], last_in, dev(x, y, z - 1, 1))

        def step_gi():
            if c == 0:
                mine = sib_send[0:SHARD]
            else:
                recv("sib", sib_in)
                mine = sib_in[...]
            recv(("last", c), last_in)
            u, u_inv = unit_rows(pic[...])
            image_dir = mine + last_in[0:SHARD].astype(jnp.float32)
            gi[...] = (image_dir - u * jnp.sum(u * image_dir, axis=1, keepdims=True)) * u_inv

        steps = dict(
            t=step_t, i=step_i, W=step_w, P=step_p, Q=step_q, pp=step_pp, b=step_b, tf=step_tf, gt=step_gt,
            ro=step_ro, rf=step_rf, la=step_la, own=step_own, gi=step_gi,
        )
        for name, *args in ORDER[c]:
            steps[name](*args)
        for cp in started:
            cp.wait_send()

    for c in (0, 1):
        pl.when(core == c)(lambda c=c: one_core(c))


def body(picture_vectors, caption_vectors, scale_exponent, score_shift):
    bf16, f32 = jnp.bfloat16, jnp.float32
    vmem = pl.BlockSpec(memory_space=pltpu.VMEM)
    smem = pl.BlockSpec(memory_space=pltpu.SMEM)
    out = jax.ShapeDtypeStruct((SHARD, D), f32)
    return pl.pallas_call(
        kernel,
        out_shape=(out, out),
        in_specs=[vmem, vmem, smem, smem],
        out_specs=(vmem, vmem),
        scratch_shapes=[
            pltpu.VMEM((SHARD, D), bf16),
            pltpu.VMEM((SHARD, D), bf16),
            pltpu.VMEM((SHARD, D), bf16),
            pltpu.VMEM((N_IMG, D), bf16),
            pltpu.VMEM((N_TXT, D), bf16),
            pltpu.VMEM((N_TXT, N_IMG), bf16),
            pltpu.VMEM((N_TXT, D), f32),
            pltpu.VMEM((N_IMG, D), f32),
            pltpu.VMEM((4, UNIT, D), bf16),
            pltpu.VMEM((4, UNIT, D), bf16),
            pltpu.VMEM((4, UNIT, D), bf16),
            pltpu.VMEM((4, UNIT, D), bf16),
            pltpu.VMEM((UNIT, D), f32),
            pltpu.VMEM((SHARD, D), f32),
            pltpu.VMEM((4, UNIT, D), bf16),
            pltpu.VMEM((8, UNIT, D), bf16),
            pltpu.VMEM((UNIT, D), bf16),
            pltpu.VMEM((2, UNIT, D), bf16),
            pltpu.VMEM((12, UNIT, D), bf16),
            pltpu.VMEM((3, UNIT, D), bf16),
            pltpu.VMEM((2, 48, D), bf16),
            pltpu.VMEM((48, D), bf16),
            pltpu.VMEM((UNIT, D), f32),
            pltpu.VMEM((SHARD, D), f32),
            pltpu.SemaphoreType.DMA((160,)),
            pltpu.SemaphoreType.DMA((160,)),
        ],
        compiler_params=pltpu.CompilerParams(
            collective_id=0, has_side_effects=True, vmem_limit_bytes=56 * 2**20
        ),
    )(picture_vectors, caption_vectors, scale_exponent, score_shift)


def solution(mesh):
    return jax.shard_map(
        body,
        mesh=mesh,
        in_specs=(P(("row", "col"), None), P(("col", "row"), None), P(), P()),
        out_specs=(P(("row", "col"), None), P(("col", "row"), None)),
        check_vma=False,
    )
```

```python
import jax
import jax.numpy as jnp
from jax import lax
from jax.experimental import pallas as pl
from jax.experimental.pallas import tpu as pltpu
from jax.sharding import PartitionSpec as P

MESH = pl.DeviceIdType.MESH
D = 1152
SHARD = 40
UNIT = 80
SLOTS = (
    (0, 0), (1, 0), (-1, 0), (2, 0), (0, 1), (0, -1), (1, 1), (1, -1),
    (-1, 1), (-1, -1), (2, 1), (2, -1), (0, 2), (1, 2), (-1, 2), (2, 2),
)
SLOT = {ab: i for i, ab in enumerate(SLOTS)}
RIGHT = (0, 2)
LINE = (0, 1, -1, 2)
N_IMG = 16 * UNIT
N_TXT = 8 * UNIT
T_ROWS = ((0, 32), (32, 32), (64, 16))
I_ROWS = ((0, 48), (48, 32))
HALF = ((0,), (1,))
FAR = ((0,), (1, 2))
T_GROUPS = ((0, 240), (240, 400), (400, 560), (560, 640))
I_GROUPS = ((0, 640), (640, 1024), (1024, 1280))
Q_GROUPS = ((896, 1280), (256, 896), (0, 256))
ORDER = (
    (
        ('i', 0, 0), ('i', 0, 1), ('t', 0, 0), ('t', 0, 2), ('t', 0, 1), ('i', 4, 0), ('i', 5, 0), ('i', 1, 0),
        ('i', 2, 0), ('i', 1, 1), ('t', 1, 0), ('i', 2, 1), ('i', 4, 1), ('i', 5, 1), ('t', 1, 2), ('t', 1, 1),
        ('i', 12, 0), ('i', 3, 1), ('i', 6, 0), ('i', 3, 0), ('t', 2, 0), ('t', 2, 2), ('i', 8, 0), ('i', 7, 0),
        ('i', 6, 1), ('t', 2, 1), ('i', 8, 1), ('i', 9, 0), ('i', 10, 1), ('i', 7, 1), ('W', 1, 0), ('t', 3, 0),
        ('W', 0, 0), ('i', 13, 0), ('i', 12, 1), ('i', 9, 1), ('t', 3, 2), ('i', 10, 0), ('i', 11, 1), ('t', 3, 1),
        ('W', 2, 0), ('i', 14, 0), ('i', 11, 0), ('W', 1, 1), ('i', 13, 1), ('W', 0, 1), ('t', 4, 0), ('i', 14, 1),
        ('W', 2, 1), ('i', 15, 1), ('W', 3, 0), ('W', 3, 1), ('i', 15, 0), ('W', 0, 2), ('W', 3, 2), ('W', 2, 2),
        ('W', 1, 2), ('Q', 0), ('ro', -1, 1), ('ro', 1, 1), ('ro', 2, 1), ('ro', 0, 0), ('ro', 2, 0), ('ro', 0, 1),
        ('ro', 1, 0), ('ro', -1, 0), ('P', 3), ('pp', 0), ('P', 2), ('b', 0, 0), ('pp', 3), ('Q', 1),
        ('rf', 2, 1, 1), ('rf', -1, -1, 1), ('rf', 1, -1, 1), ('rf', 2, -1, 0), ('rf', 0, -1, 0), ('rf', -1, 1, 0),
        ('rf', 0, 1, 0), ('rf', 1, 1, 0), ('rf', 2, -1, 1), ('rf', 1, 1, 1), ('rf', 0, -1, 1), ('Q', 2), ('b', 3, 2),
        ('b', 3, 1), ('rf', 2, 1, 0), ('rf', 1, -1, 0), ('P', 0), ('rf', 0, 1, 1), ('pp', 1), ('b', 3, 0),
        ('rf', -1, -1, 0), ('P', 1), ('pp', 2), ('rf', -1, 1, 1), ('b', 2, 2), ('b', 2, 1), ('la', 2, 1),
        ('la', 1, 1), ('b', 2, 0), ('b', 1, 2), ('la', 2, 0), ('b', 1, 1), ('la', -1, 0), ('la', -1, 1), ('b', 1, 0),
        ('la', 1, 0), ('own',), ('tf',), ('gi',), ('gt',),
    ),
    (
        ('t', 0, 1), ('t', 0, 0), ('t', 0, 2), ('i', 0, 0), ('i', 0, 1), ('t', 1, 1), ('t', 1, 0), ('t', 1, 2),
        ('i', 4, 0), ('i', 5, 0), ('i', 2, 0), ('i', 1, 0), ('i', 4, 1), ('i', 5, 1), ('t', 2, 1), ('i', 1, 1),
        ('i', 2, 1), ('t', 2, 0), ('i', 12, 0), ('i', 8, 0), ('t', 2, 2), ('i', 9, 0), ('i', 3, 0), ('i', 6, 0),
        ('i', 3, 1), ('i', 6, 1), ('i', 7, 0), ('t', 3, 1), ('i', 12, 1), ('i', 8, 1), ('i', 7, 1), ('W', 0, 0),
        ('t', 3, 0), ('i', 14, 0), ('i', 9, 1), ('t', 3, 2), ('W', 1, 0), ('i', 10, 0), ('i', 11, 0), ('W', 2, 0),
        ('t', 4, 1), ('i', 13, 0), ('i', 11, 1), ('i', 10, 1), ('W', 2, 1), ('W', 1, 1), ('W', 0, 1), ('t', 4, 2),
        ('i', 13, 1), ('W', 3, 0), ('i', 14, 1), ('W', 3, 1), ('i', 15, 0), ('Q', 1), ('rf', 0, -1, 0),
        ('rf', 1, 1, 0), ('rf', 0, -1, 1), ('rf', 1, 1, 1), ('rf', -1, 1, 1), ('i', 15, 1), ('W', 2, 2), ('W', 3, 2),
        ('rf', -1, 1, 0), ('W', 1, 2), ('W', 0, 2), ('P', 3), ('pp', 0), ('Q', 0), ('ro', 1, 0), ('ro', 1, 1),
        ('ro', -1, 0), ('ro', 2, 0), ('ro', 2, 1), ('ro', 0, 0), ('ro', -1, 1), ('rf', 2, -1, 1), ('rf', 2, -1, 0),
        ('ro', 0, 1), ('b', 0, 1), ('b', 0, 2), ('P', 2), ('pp', 3), ('b', 3, 0), ('P', 0), ('pp', 1),
        ('rf', 1, -1, 0), ('P', 1), ('rf', 1, -1, 1), ('rf', 2, 1, 0), ('pp', 2), ('Q', 2), ('b', 3, 1),
        ('rf', -1, -1, 0), ('rf', 2, 1, 1), ('b', 3, 2), ('rf', -1, -1, 1), ('rf', 0, 1, 0), ('rf', 0, 1, 1),
        ('b', 2, 0), ('la', 2, 0), ('la', 2, 1), ('b', 2, 1), ('la', 1, 1), ('b', 2, 2), ('la', -1, 0), ('b', 1, 0),
        ('la', 1, 0), ('la', -1, 1), ('b', 1, 1), ('b', 1, 2), ('own',), ('tf',), ('gt',), ('gi',),
    ),
)


def unit_rows(values):
    values = values.astype(jnp.float32)
    inverse = lax.rsqrt(jnp.sum(values * values, axis=1, keepdims=True) + 1e-06)
    return values * inverse, inverse


def kernel(
    pic, cap, scale, shift, gi, gt,
    raw_cap, raw_a, raw_b, img, txt, wt, pbuf, qbuf,
    psend, pd, rsb, rr, tf, tfr,
    rel_in, fin_in, half_in, afin_in, bsend, asend, last_send, last_in, sib_send, sib_in,
    ssem, rsem,
):
    r = lax.axis_index("row")
    q = lax.axis_index("col")
    x, y, z, core = (q % 8) // 2, r // 8, (q // 8) * 8 + r % 8, q % 2

    def dev(x, y, z, c):
        x, y, z = (x + 4) % 4, (y + 4) % 4, (z + 16) % 16
        return (y * 8 + z % 8, (z // 8) * 8 + x * 2 + c)

    barrier = pltpu.get_barrier_semaphore()

    def greet(to):
        pl.semaphore_signal(barrier, inc=1, device_id=to, device_id_type=MESH)

    for to in (
        dev(x, y, z, 1 - core), dev(x + 1, y, z, core), dev(x - 1, y, z, core), dev(x, y + 1, z, core),
        dev(x, y - 1, z, core), dev(x, y, z + 2, core), dev(x, y, z - 2, core), dev(x, y, z + 1, 1),
    ):
        greet(to)

    @pl.when(core == 1)
    def _():
        greet(dev(x, y, z - 1, 1))
        greet(dev(x, y, z - 1, 0))

    ids = {}
    offset = shift[0]

    def one_core(c):
        sib = dev(x, y, z, 1 - c)
        sg = 1 - 2 * c
        ahead = dev(x, y, z + 2 * sg, c)
        behind = dev(x, y, z - 2 * sg, c)
        started = []

        def along_a(s):
            return dev(x + s * (1 - c), y + s * c, z, c)

        def along_b(s):
            return dev(x + s * c, y + s * (1 - c), z, c)

        def rcopy(key, src, dst, to):
            i = ids.setdefault(key, len(ids))
            return pltpu.make_async_remote_copy(
                src_ref=src, dst_ref=dst, send_sem=ssem.at[i], recv_sem=rsem.at[i],
                device_id=to, device_id_type=MESH,
            )

        def send(key, src, dst, to):
            cp = rcopy(key, src, dst, to)
            cp.start()
            started.append(cp)

        def recv(key, dst):
            rcopy(key, dst, dst, sib).wait_recv()

        smooth = jnp.exp(jnp.full((1, 128), scale[0], jnp.float32))[:, :1]
        lane = lax.broadcasted_iota(jnp.int32, (1, N_IMG), 1)
        zi = (z - c + 16) % 16
        img_ids = lane
        before = None
        for s, (a, b) in enumerate(SLOTS):
            xs = (x + a * (1 - c) + b * c + 4) % 4
            ys = (y + a * c + b * (1 - c) + 4) % 4
            base = ((ys * 8 + zi % 8) * 16 + (zi // 8) * 8 + xs * 2) * SHARD
            if s == 0:
                img_ids = img_ids + base
            else:
                img_ids = img_ids + jnp.where(lane >= s * UNIT, base - before - UNIT, 0)
            before = base
        row_in = lax.broadcasted_iota(jnp.int32, (UNIT, 1), 0)
        row_in = row_in + jnp.where(row_in >= SHARD, 32 * SHARD - SHARD, 0)

        def txt_ids(slot):
            step = 0 if slot == 0 else (8 if slot == 7 else (-2 * ((slot + 1) // 2) if slot % 2 else slot))
            zt = (z + step + 16) % 16
            return row_in + (((zt // 8) * 8 + x * 2) * 32 + y * 8 + zt % 8) * SHARD

        own_txt = unit_rows(cap[...])[0]
        if c == 0:
            own_img = unit_rows(pic[...])[0]
        pl.semaphore_wait(barrier, 10 if c else 8)
        send("cap", cap, raw_cap, sib)
        if c == 0:
            send("pic_a", pic, raw_a, dev(x, y, z + 1, 1))
        else:
            send("pic_0", pic, raw_a, sib)
            send("pic_b", pic, raw_b, dev(x, y, z + 1, 1))

        def both(one, two):
            return jnp.concatenate([one, two], axis=0).astype(jnp.bfloat16)

        def f_slot(k):
            return 0 if k == 0 else (7 if k == 4 else 2 * k - 1 + c)

        def g_slot(k):
            return 7 if k == 4 else 2 * k - c

        def t_piece(slot, h):
            return pl.ds(slot * UNIT + T_ROWS[h][0], T_ROWS[h][1])

        def i_piece(slot, h):
            return pl.ds(slot * UNIT + I_ROWS[h][0], I_ROWS[h][1])

        got = set()

        def need(key, dst):
            if key not in got:
                got.add(key)
                recv(key, dst)

        def step_t(k, h):
            if k == 0:
                if "txt" not in got:
                    got.add("txt")
                    recv("cap", raw_cap)
                    other = unit_rows(raw_cap[...])[0]
                    txt[0:UNIT] = both(own_txt, other) if c == 0 else both(other, own_txt)
            else:
                need(("t", k, h), txt.at[t_piece(f_slot(k), h)])
            here = txt.at[t_piece(f_slot(k), h)]
            if k < 3 or (k == 3 and h in FAR[c]):
                send(("t", k + 1, h), here, txt.at[t_piece(f_slot(k + 1), h)], ahead)
            if k > 0:
                send(("g", k, h), here, here, sib)

        def step_i(s, h):
            a, b = SLOTS[s]

            def forward(to_slot, to):
                send(("i", to_slot, h), img.at[i_piece(s, h)], img.at[i_piece(to_slot, h)], to)

            if s == 0:
                if "img" not in got:
                    got.add("img")
                    if c == 0:
                        recv("pic_0", raw_a)
                        img[0:UNIT] = both(own_img, unit_rows(raw_a[...])[0])
                    else:
                        recv("pic_a", raw_a)
                        recv("pic_b", raw_b)
                        img[0:UNIT] = both(unit_rows(raw_a[...])[0], unit_rows(raw_b[...])[0])
                forward(SLOT[-1, 0], along_a(1))
                forward(SLOT[1, 0], along_a(-1))
            else:
                need(("i", s, h), img.at[i_piece(s, h)])
            if b == 0:
                if a == -1 and h in HALF[0]:
                    forward(SLOT[2, 0], along_a(1))
                if a == 1 and h in HALF[1]:
                    forward(SLOT[2, 0], along_a(-1))
                forward(SLOT[a, -1], along_b(1))
                forward(SLOT[a, 1], along_b(-1))
            if b == -1 and a in RIGHT:
                forward(SLOT[a, 2], along_b(1))
            if b == 1 and a not in RIGHT:
                forward(SLOT[a, 2], along_b(-1))

        def text_needs(slot):
            if slot == 0:
                return
            k = 4 if slot == 7 else (slot + 1) // 2
            for h in range(len(T_ROWS)):
                mine = h in FAR[c] if k == 4 else (slot % 2 == 1) == (c == 0)
                if not mine:
                    need(("g", k, h), txt.at[t_piece(slot, h)])

        def step_w(gt_, gi_):
            t0, t1 = T_GROUPS[gt_]
            i0, i1 = I_GROUPS[gi_]
            for s in range(t0 // UNIT, t1 // UNIT):
                text_needs(s)
            dots = lax.dot_general(
                txt[t0:t1], img[i0:i1], (((1,), (1,)), ((), ())), preferred_element_type=jnp.float32
            )
            logits = smooth * dots + offset
            tid = jnp.concatenate([txt_ids(s) for s in range(t0 // UNIT, t1 // UNIT)], axis=0)
            match = tid == img_ids[:, i0:i1]
            value = smooth / (1.0 + jnp.exp(jnp.where(match, logits, -logits)))
            wt[t0:t1, i0:i1] = jnp.where(match, -value, value).astype(jnp.bfloat16)

        def step_p(g):
            t0, t1 = T_GROUPS[g]
            pbuf[t0:t1] = jnp.dot(wt[t0:t1], img[...], preferred_element_type=jnp.float32)

        def step_q(g):
            i0, i1 = Q_GROUPS[g]
            qbuf[i0:i1] = lax.dot_general(
                wt[:, i0:i1], txt[...], (((0,), (0,)), ((), ())), preferred_element_type=jnp.float32
            )

        def step_pp(k):
            slot = g_slot(k) if k else 7
            psend[k] = pbuf[slot * UNIT:(slot + 1) * UNIT].astype(jnp.bfloat16)
            for h, (o, n) in enumerate(T_ROWS):
                if k > 0 or h in FAR[1 - c]:
                    send(("p", k, h), psend.at[k, pl.ds(o, n)], pd.at[k, pl.ds(o, n)], sib)

        def step_b(k, h):
            o, n = T_ROWS[h]
            slot = f_slot(k) if k else 7
            recv(("p", k, h), pd.at[k, pl.ds(o, n)])
            total = pbuf[slot * UNIT + o:slot * UNIT + o + n] + pd[k, o:o + n].astype(jnp.float32)
            more = {3: 0, 2: 3, 1: 2}.get(k)
            if k in (1, 2) or (k == 3 and h in FAR[c]):
                recv(("b", more, h), rr.at[k, pl.ds(o, n)])
                total = total + rr[k, o:o + n].astype(jnp.float32)
            rsb[k, o:o + n] = total.astype(jnp.bfloat16)
            to = 3 if k == 0 else k - 1
            send(("b", k, h), rsb.at[k, pl.ds(o, n)], rr.at[to, pl.ds(o, n)], behind)

        def step_tf():
            for h, (o, n) in enumerate(T_ROWS):
                recv(("b", 1, h), rr.at[0, pl.ds(o, n)])
            tf[...] = pbuf[0:UNIT] + rr[0].astype(jnp.float32)
            send("tf", tf.at[pl.ds((1 - c) * SHARD, SHARD)], tfr, sib)

        def step_gt():
            recv("tf", tfr)
            v, v_inv = unit_rows(cap[...])
            text_dir = tf[c * SHARD:(c + 1) * SHARD] + tfr[...]
            gt[...] = (text_dir - v * jnp.sum(v * text_dir, axis=1, keepdims=True)) * v_inv

        def q_piece(slot, h):
            o, n = I_ROWS[h]
            return qbuf[slot * UNIT + o:slot * UNIT + o + n]

        def step_ro(a, h):
            n = LINE.index(a)
            o, m = I_ROWS[h]
            bsend[n, o:o + m] = q_piece(SLOT[a, 2], h).astype(jnp.bfloat16)
            here = pl.ds(o, m)
            send(("ro", a, h), bsend.at[n, here], rel_in.at[n, here], along_b(1 if a in RIGHT else -1))

        def step_rf(a, s, h):
            n = LINE.index(a)
            o, m = I_ROWS[h]
            here = pl.ds(o, m)
            total = q_piece(SLOT[a, s], h)
            if (a in RIGHT) == (s == 1):
                recv(("ro", a, h), rel_in.at[n, here])
                total = total + rel_in[n, o:o + m].astype(jnp.float32)
            to = n if s == 1 else 4 + n
            bsend[4 + to, o:o + m] = total.astype(jnp.bfloat16)
            send(("rf", a, s, h), bsend.at[4 + to, here], fin_in.at[to, here], along_b(s))

        def line_total(a, h):
            n = LINE.index(a)
            o, m = I_ROWS[h]
            here = pl.ds(o, m)
            recv(("rf", a, 1, h), fin_in.at[n, here])
            recv(("rf", a, -1, h), fin_in.at[4 + n, here])
            return (
                q_piece(SLOT[a, 0], h)
                + fin_in[n, o:o + m].astype(jnp.float32)
                + fin_in[4 + n, o:o + m].astype(jnp.float32)
            )

        def step_la(a, h):
            o, m = I_ROWS[h]
            here = pl.ds(o, m)
            total = line_total(a, h)
            i = {2: 0, 1: 1, -1: 2}[a]
            if (a == 1 and h in HALF[0]) or (a == -1 and h in HALF[1]):
                recv(("ra", h), half_in.at[here])
                total = total + half_in[o:o + m].astype(jnp.float32)
            asend[i, o:o + m] = total.astype(jnp.bfloat16)
            if a == 2:
                send(("ra", h), asend.at[i, here], half_in.at[here], along_a(1 if h in HALF[0] else -1))
            else:
                send(("rb", a, h), asend.at[i, here], afin_in.at[i - 1, here], along_a(a))

        def step_own():
            parts = []
            for h, (o, m) in enumerate(I_ROWS):
                total = line_total(0, h)
                for i, a in enumerate((1, -1)):
                    recv(("rb", a, h), afin_in.at[i, pl.ds(o, m)])
                    total = total + afin_in[i, o:o + m].astype(jnp.float32)
                parts.append(total)
            own = jnp.concatenate(parts, axis=0)
            if c == 0:
                sib_send[...] = own
                send("sib", sib_send.at[pl.ds(SHARD, SHARD)], sib_in, sib)
            else:
                for h in range(2):
                    last_send[h, 0:SHARD] = own[h * SHARD:(h + 1) * SHARD].astype(jnp.bfloat16)
                    last_send[h, SHARD:48] = jnp.zeros((48 - SHARD, D), jnp.bfloat16)
                send(("last", 0), last_send.at[0], last_in, dev(x, y, z - 1, 0))
                send(("last", 1), last_send.at[1], last_in, dev(x, y, z - 1, 1))

        def step_gi():
            if c == 0:
                mine = sib_send[0:SHARD]
            else:
                recv("sib", sib_in)
                mine = sib_in[...]
            recv(("last", c), last_in)
            u, u_inv = unit_rows(pic[...])
            image_dir = mine + last_in[0:SHARD].astype(jnp.float32)
            gi[...] = (image_dir - u * jnp.sum(u * image_dir, axis=1, keepdims=True)) * u_inv

        steps = dict(
            t=step_t, i=step_i, W=step_w, P=step_p, Q=step_q, pp=step_pp, b=step_b, tf=step_tf, gt=step_gt,
            ro=step_ro, rf=step_rf, la=step_la, own=step_own, gi=step_gi,
        )
        for name, *args in ORDER[c]:
            steps[name](*args)
        for cp in started:
            cp.wait_send()

    for c in (0, 1):
        pl.when(core == c)(lambda c=c: one_core(c))


def body(picture_vectors, caption_vectors, scale_exponent, score_shift):
    bf16, f32 = jnp.bfloat16, jnp.float32
    vmem = pl.BlockSpec(memory_space=pltpu.VMEM)
    smem = pl.BlockSpec(memory_space=pltpu.SMEM)
    out = jax.ShapeDtypeStruct((SHARD, D), f32)
    return pl.pallas_call(
        kernel,
        out_shape=(out, out),
        in_specs=[vmem, vmem, smem, smem],
        out_specs=(vmem, vmem),
        scratch_shapes=[
            pltpu.VMEM((SHARD, D), bf16),
            pltpu.VMEM((SHARD, D), bf16),
            pltpu.VMEM((SHARD, D), bf16),
            pltpu.VMEM((N_IMG, D), bf16),
            pltpu.VMEM((N_TXT, D), bf16),
            pltpu.VMEM((N_TXT, N_IMG), bf16),
            pltpu.VMEM((N_TXT, D), f32),
            pltpu.VMEM((N_IMG, D), f32),
            pltpu.VMEM((4, UNIT, D), bf16),
            pltpu.VMEM((4, UNIT, D), bf16),
            pltpu.VMEM((4, UNIT, D), bf16),
            pltpu.VMEM((4, UNIT, D), bf16),
            pltpu.VMEM((UNIT, D), f32),
            pltpu.VMEM((SHARD, D), f32),
            pltpu.VMEM((4, UNIT, D), bf16),
            pltpu.VMEM((8, UNIT, D), bf16),
            pltpu.VMEM((UNIT, D), bf16),
            pltpu.VMEM((2, UNIT, D), bf16),
            pltpu.VMEM((12, UNIT, D), bf16),
            pltpu.VMEM((3, UNIT, D), bf16),
            pltpu.VMEM((2, 48, D), bf16),
            pltpu.VMEM((48, D), bf16),
            pltpu.VMEM((UNIT, D), f32),
            pltpu.VMEM((SHARD, D), f32),
            pltpu.SemaphoreType.DMA((160,)),
            pltpu.SemaphoreType.DMA((160,)),
        ],
        compiler_params=pltpu.CompilerParams(
            collective_id=0, has_side_effects=True, vmem_limit_bytes=34 * 2**20
        ),
    )(picture_vectors, caption_vectors, scale_exponent, score_shift)


def solution(mesh):
    return jax.shard_map(
        body,
        mesh=mesh,
        in_specs=(P(("row", "col"), None), P(("col", "row"), None), P(), P()),
        out_specs=(P(("row", "col"), None), P(("col", "row"), None)),
        check_vma=False,
    )
```

```python
import jax
import jax.numpy as jnp
from jax import lax
from jax.experimental import pallas as pl
from jax.experimental.pallas import tpu as pltpu
from jax.sharding import PartitionSpec as P

MESH = pl.DeviceIdType.MESH
D = 1152
SHARD = 40
UNIT = 80
SLOTS = (
    (0, 0), (1, 0), (-1, 0), (2, 0), (0, 1), (0, -1), (1, 1), (1, -1),
    (-1, 1), (-1, -1), (2, 1), (2, -1), (0, 2), (1, 2), (-1, 2), (2, 2),
)
SLOT = {ab: i for i, ab in enumerate(SLOTS)}
RIGHT = (0, 2)
LINE = (0, 1, -1, 2)
N_IMG = 16 * UNIT
N_TXT = 8 * UNIT
T_ROWS = ((0, 32), (32, 16), (48, 32))
I_ROWS = ((0, 32), (32, 16), (48, 32))
HALF = ((0, 1), (2,))
FAR = ((1,), (0, 2))
ROUTE = ({}, {})
DIRECT = ()
T_GROUPS = ((0, 240), (240, 400), (400, 560), (560, 640))
I_GROUPS = ((0, 640), (640, 1024), (1024, 1280))
Q_GROUPS = ((896, 1280), (256, 896), (0, 256))
ORDER = (
    (
        ('t', 0, 0), ('t', 0, 1), ('t', 0, 2), ('i', 0, 2), ('i', 0, 0), ('i', 0, 1), ('i', 5, 2), ('i', 4, 2),
        ('i', 1, 2), ('i', 2, 2), ('i', 2, 0), ('t', 1, 0), ('i', 1, 0), ('i', 5, 1), ('i', 1, 1), ('i', 4, 0),
        ('i', 5, 0), ('t', 1, 1), ('i', 2, 1), ('i', 4, 1), ('t', 1, 2), ('i', 12, 2), ('i', 6, 2), ('i', 3, 2),
        ('i', 3, 0), ('i', 7, 2), ('t', 2, 0), ('i', 3, 1), ('i', 8, 2), ('t', 2, 1), ('i', 8, 0), ('i', 9, 2),
        ('i', 6, 0), ('i', 6, 1), ('t', 2, 2), ('i', 8, 1), ('i', 9, 0), ('i', 7, 0), ('i', 13, 2), ('t', 3, 0),
        ('i', 12, 1), ('i', 7, 1), ('W', 1, 0), ('t', 3, 1), ('i', 10, 2), ('i', 12, 0), ('W', 0, 0), ('i', 10, 0),
        ('i', 10, 1), ('i', 9, 1), ('i', 11, 2), ('t', 3, 2), ('i', 14, 2), ('i', 11, 0), ('i', 14, 0), ('i', 11, 1),
        ('W', 1, 1), ('W', 2, 1), ('i', 13, 0), ('W', 0, 1), ('t', 4, 1), ('i', 13, 1), ('i', 14, 1), ('W', 2, 0),
        ('i', 15, 2), ('i', 15, 0), ('i', 15, 1), ('W', 1, 2), ('W', 0, 2), ('W', 2, 2), ('W', 3, 1), ('W', 3, 0),
        ('W', 3, 2), ('P', 3), ('pp', 0), ('P', 2), ('pp', 3), ('Q', 0), ('ro', 2, 1), ('b', 3, 0), ('b', 3, 2),
        ('ro', -1, 2), ('ro', 2, 0), ('ro', 2, 2), ('ro', -1, 1), ('ro', 1, 0), ('ro', -1, 0), ('ro', 0, 2),
        ('ro', 0, 0), ('ro', 1, 2), ('ro', 1, 1), ('b', 0, 1), ('ro', 0, 1), ('P', 1), ('pp', 2), ('Q', 1),
        ('rf', 2, 1, 0), ('rf', 2, -1, 2), ('rf', 0, -1, 1), ('rf', -1, 1, 0), ('rf', 1, 1, 0), ('rf', 1, 1, 1),
        ('rf', 1, 1, 2), ('rf', 2, -1, 0), ('rf', 0, -1, 0), ('b', 2, 0), ('rf', 2, 1, 2), ('rf', -1, 1, 1),
        ('rf', 1, -1, 0), ('rf', 2, 1, 1), ('rf', 2, -1, 1), ('rf', -1, 1, 2), ('rf', -1, -1, 1), ('rf', 0, -1, 2),
        ('rf', 0, 1, 2), ('rf', -1, -1, 2), ('P', 0), ('pp', 1), ('b', 3, 1), ('po',), ('b', 2, 2), ('rf', 1, -1, 2),
        ('rf', 0, 1, 1), ('rf', -1, -1, 0), ('rf', 1, -1, 1), ('rf', 0, 1, 0), ('Q', 2), ('la', 2, 0), ('b', 1, 0),
        ('b', 2, 1), ('la', 2, 2), ('b', 1, 2), ('la', -1, 1), ('la', 2, 1), ('la', 1, 0), ('b', 1, 1),
        ('la', -1, 2), ('la', 1, 2), ('la', -1, 0), ('la', 1, 1), ('gt',), ('own', 2), ('own', 1), ('own', 0),
        ('gi',),
    ),
    (
        ('t', 0, 0), ('t', 0, 2), ('t', 0, 1), ('i', 0, 0), ('i', 0, 1), ('i', 0, 2), ('t', 1, 0), ('t', 1, 2),
        ('i', 4, 0), ('i', 1, 0), ('i', 5, 0), ('t', 1, 1), ('i', 5, 1), ('i', 2, 0), ('i', 1, 1), ('i', 4, 1),
        ('i', 2, 1), ('i', 5, 2), ('i', 4, 2), ('t', 2, 0), ('i', 1, 2), ('i', 2, 2), ('i', 7, 0), ('i', 6, 0),
        ('t', 2, 2), ('i', 8, 0), ('i', 12, 0), ('i', 3, 0), ('i', 12, 1), ('i', 6, 1), ('t', 2, 1), ('i', 8, 1),
        ('i', 3, 1), ('i', 9, 0), ('i', 7, 1), ('i', 6, 2), ('i', 9, 1), ('i', 3, 2), ('i', 8, 2), ('t', 3, 0),
        ('i', 12, 2), ('i', 13, 0), ('i', 7, 2), ('W', 1, 0), ('i', 14, 0), ('t', 3, 2), ('i', 9, 2), ('W', 0, 0),
        ('i', 11, 0), ('i', 13, 1), ('t', 3, 1), ('i', 10, 0), ('i', 14, 1), ('i', 11, 1), ('i', 10, 1),
        ('i', 11, 2), ('W', 2, 0), ('t', 4, 0), ('i', 13, 2), ('i', 10, 2), ('W', 2, 1), ('W', 1, 1), ('W', 0, 1),
        ('i', 15, 0), ('i', 14, 2), ('t', 4, 2), ('W', 3, 0), ('i', 15, 1), ('W', 3, 1), ('i', 15, 2), ('W', 0, 2),
        ('W', 2, 2), ('W', 3, 2), ('W', 1, 2), ('P', 2), ('pp', 3), ('P', 3), ('pp', 0), ('Q', 0), ('b', 0, 0),
        ('ro', 2, 0), ('ro', 1, 1), ('ro', 2, 2), ('ro', 2, 1), ('ro', 1, 0), ('ro', -1, 0), ('b', 0, 2),
        ('ro', -1, 1), ('ro', 0, 2), ('b', 3, 1), ('ro', 1, 2), ('ro', 0, 0), ('ro', 0, 1), ('ro', -1, 2), ('P', 1),
        ('pp', 2), ('Q', 1), ('rf', -1, 1, 1), ('rf', 2, 1, 0), ('rf', 2, -1, 0), ('rf', 0, -1, 2), ('rf', 2, -1, 2),
        ('rf', 2, -1, 1), ('rf', 2, 1, 2), ('rf', 1, 1, 2), ('rf', -1, 1, 0), ('rf', 1, -1, 0), ('rf', 2, 1, 1),
        ('rf', 1, 1, 0), ('rf', 0, -1, 1), ('rf', 1, 1, 1), ('rf', -1, 1, 2), ('rf', -1, -1, 1), ('rf', -1, -1, 0),
        ('rf', 0, -1, 0), ('b', 3, 0), ('rf', 0, 1, 2), ('rf', 1, -1, 1), ('Q', 2), ('b', 3, 2), ('rf', 0, 1, 0),
        ('rf', 1, -1, 2), ('P', 0), ('rf', 0, 1, 1), ('pp', 1), ('la', 2, 0), ('rf', -1, -1, 2), ('b', 2, 1),
        ('po',), ('la', 2, 2), ('b', 2, 0), ('la', 2, 1), ('la', -1, 1), ('b', 2, 2), ('la', 1, 0), ('la', -1, 0),
        ('b', 1, 1), ('la', 1, 1), ('la', 1, 2), ('b', 1, 0), ('la', -1, 2), ('b', 1, 2), ('own', 0), ('own', 1),
        ('own', 2), ('gt',), ('gi',),
    ),
)


def unit_rows(values):
    values = values.astype(jnp.float32)
    inverse = lax.rsqrt(jnp.sum(values * values, axis=1, keepdims=True) + 1e-06)
    return values * inverse, inverse


def kernel(
    raw, scale, shift, grads,
    raw_cap, raw_a, raw_b, img, txt, wt, pbuf, qbuf,
    psend, pd, rsb, rr, own_in, other,
    rel_in, fin_in, half_in, afin_in, bsend, asend, last_send, last_in, own_buf, sib_in,
    ssem, rsem,
):
    r = lax.axis_index("row")
    q = lax.axis_index("col")
    x, y, z, core = (q % 8) // 2, r // 8, (q // 8) * 8 + r % 8, q % 2

    def dev(x, y, z, c):
        x, y, z = (x + 4) % 4, (y + 4) % 4, (z + 16) % 16
        return (y * 8 + z % 8, (z // 8) * 8 + x * 2 + c)

    barrier = pltpu.get_barrier_semaphore()

    def greet(to):
        pl.semaphore_signal(barrier, inc=1, device_id=to, device_id_type=MESH)

    for to in (
        dev(x, y, z, 1 - core), dev(x + 1, y, z, core), dev(x - 1, y, z, core), dev(x, y + 1, z, core),
        dev(x, y - 1, z, core), dev(x, y, z + 2, core), dev(x, y, z - 2, core), dev(x, y, z + 1, 1),
        dev(x, y, z - 2 + 4 * core, 1 - core),
    ):
        greet(to)

    @pl.when(core == 1)
    def _():
        greet(dev(x, y, z - 1, 1))
        greet(dev(x, y, z - 1, 0))

    for c in DIRECT:
        @pl.when(core == c)
        def _(c=c):
            greet(dev(x + 2 * (1 - c), y + 2 * c, z, c))

    pic, cap = raw.at[0], raw.at[1]
    ids = {}
    offset = shift[0]

    def one_core(c):
        sib = dev(x, y, z, 1 - c)
        sg = 1 - 2 * c
        ahead = dev(x, y, z + 2 * sg, c)
        behind = dev(x, y, z - 2 * sg, c)
        started = []

        def along_a(s):
            return dev(x + s * (1 - c), y + s * c, z, c)

        def along_b(s):
            return dev(x + s * c, y + s * (1 - c), z, c)

        def rcopy(key, src, dst, to):
            i = ids.setdefault(key, len(ids))
            return pltpu.make_async_remote_copy(
                src_ref=src, dst_ref=dst, send_sem=ssem.at[i], recv_sem=rsem.at[i],
                device_id=to, device_id_type=MESH,
            )

        def send(key, src, dst, to):
            cp = rcopy(key, src, dst, to)
            cp.start()
            started.append(cp)

        def recv(key, dst):
            rcopy(key, dst, dst, sib).wait_recv()

        smooth = jnp.exp(jnp.full((1, 128), scale[0], jnp.float32))[:, :1]
        lane = lax.broadcasted_iota(jnp.int32, (1, N_IMG), 1)
        zi = (z - c + 16) % 16
        img_ids = lane
        before = None
        for s, (a, b) in enumerate(SLOTS):
            xs = (x + a * (1 - c) + b * c + 4) % 4
            ys = (y + a * c + b * (1 - c) + 4) % 4
            base = ((ys * 8 + zi % 8) * 16 + (zi // 8) * 8 + xs * 2) * SHARD
            if s == 0:
                img_ids = img_ids + base
            else:
                img_ids = img_ids + jnp.where(lane >= s * UNIT, base - before - UNIT, 0)
            before = base
        row_in = lax.broadcasted_iota(jnp.int32, (UNIT, 1), 0)
        row_in = row_in + jnp.where(row_in >= SHARD, 32 * SHARD - SHARD, 0)

        def txt_ids(slot):
            step = 0 if slot == 0 else (8 if slot == 7 else (-2 * ((slot + 1) // 2) if slot % 2 else slot))
            zt = (z + step + 16) % 16
            return row_in + (((zt // 8) * 8 + x * 2) * 32 + y * 8 + zt % 8) * SHARD

        pl.semaphore_wait(barrier, (11 if c else 9) + (1 if c in DIRECT else 0))
        send("cap", cap, raw_cap, sib)
        if c == 0:
            send("pic_a", pic, raw_a, dev(x, y, z + 1, 1))
        else:
            send("pic_0", pic, raw_a, sib)
            send("pic_b", pic, raw_b, dev(x, y, z + 1, 1))
        own_txt = unit_rows(cap[...])[0]
        if c == 0:
            own_img = unit_rows(pic[...])[0]

        def both(one, two):
            return jnp.concatenate([one, two], axis=0).astype(jnp.bfloat16)

        def f_slot(k):
            return 0 if k == 0 else (7 if k == 4 else 2 * k - 1 + c)

        def g_slot(k):
            return 7 if k == 4 else 2 * k - c

        def t_piece(slot, h):
            return pl.ds(slot * UNIT + T_ROWS[h][0], T_ROWS[h][1])

        def i_piece(slot, h):
            return pl.ds(slot * UNIT + I_ROWS[h][0], I_ROWS[h][1])

        got = set()

        def need(key, dst):
            if key not in got:
                got.add(key)
                recv(key, dst)

        def step_t(k, h):
            if k == 0:
                if "txt" not in got:
                    got.add("txt")
                    recv("cap", raw_cap)
                    other = unit_rows(raw_cap[...])[0]
                    txt[0:UNIT] = both(own_txt, other) if c == 0 else both(other, own_txt)
            else:
                need(("t", k, h), txt.at[t_piece(f_slot(k), h)])
            here = txt.at[t_piece(f_slot(k), h)]
            if k < 3 or (k == 3 and h in FAR[c]):
                send(("t", k + 1, h), here, txt.at[t_piece(f_slot(k + 1), h)], ahead)
            if k > 0:
                send(("g", k, h), here, here, sib)

        def step_i(s, h):
            a, b = SLOTS[s]

            def forward(to_slot, to):
                send(("i", to_slot, h), img.at[i_piece(s, h)], img.at[i_piece(to_slot, h)], to)

            if s == 0:
                if "img" not in got:
                    got.add("img")
                    if c == 0:
                        recv("pic_0", raw_a)
                        img[0:UNIT] = both(own_img, unit_rows(raw_a[...])[0])
                    else:
                        recv("pic_a", raw_a)
                        recv("pic_b", raw_b)
                        img[0:UNIT] = both(unit_rows(raw_a[...])[0], unit_rows(raw_b[...])[0])
                forward(SLOT[-1, 0], along_a(1))
                forward(SLOT[1, 0], along_a(-1))
            else:
                need(("i", s, h), img.at[i_piece(s, h)])
            if b == 0:
                if a == -1 and h in HALF[0] and c not in DIRECT:
                    forward(SLOT[2, 0], along_a(1))
                if a == 1 and h in HALF[1] and c not in DIRECT:
                    forward(SLOT[2, 0], along_a(-1))
                forward(SLOT[a, -1], along_b(1))
                forward(SLOT[a, 1], along_b(-1))
                if a == 0 and c in DIRECT:
                    forward(SLOT[2, 0], along_a(2))

            def way(a):
                return ROUTE[c].get((a, h), (0, 1) if a in RIGHT else (0, -1))

            if abs(b) == 1 and way(a) == (0, -b):
                forward(SLOT[a, 2], along_b(-b))
            if (a, b) == (0, 2):
                for s_a in (-1, 1):
                    if way(s_a) == (-s_a, 0):
                        forward(SLOT[s_a, 2], along_a(-s_a))

        def text_needs(slot):
            if slot == 0:
                return
            k = 4 if slot == 7 else (slot + 1) // 2
            for h in range(len(T_ROWS)):
                mine = h in FAR[c] if k == 4 else (slot % 2 == 1) == (c == 0)
                if not mine:
                    need(("g", k, h), txt.at[t_piece(slot, h)])

        def step_w(gt_, gi_):
            t0, t1 = T_GROUPS[gt_]
            i0, i1 = I_GROUPS[gi_]
            for s in range(t0 // UNIT, t1 // UNIT):
                text_needs(s)
            dots = lax.dot_general(
                txt[t0:t1], img[i0:i1], (((1,), (1,)), ((), ())), preferred_element_type=jnp.float32
            )
            logits = smooth * dots + offset
            tid = jnp.concatenate([txt_ids(s) for s in range(t0 // UNIT, t1 // UNIT)], axis=0)
            match = tid == img_ids[:, i0:i1]
            value = smooth / (1.0 + jnp.exp(jnp.where(match, logits, -logits)))
            wt[t0:t1, i0:i1] = jnp.where(match, -value, value).astype(jnp.bfloat16)

        def step_p(g):
            t0, t1 = T_GROUPS[g]
            pbuf[t0:t1] = jnp.dot(wt[t0:t1], img[...], preferred_element_type=jnp.float32)

        def step_q(g):
            i0, i1 = Q_GROUPS[g]
            qbuf[i0:i1] = lax.dot_general(
                wt[:, i0:i1], txt[...], (((0,), (0,)), ((), ())), preferred_element_type=jnp.float32
            )

        def step_pp(k):
            slot = g_slot(k) if k else 7
            psend[k] = pbuf[slot * UNIT:(slot + 1) * UNIT].astype(jnp.bfloat16)
            for h, (o, n) in enumerate(T_ROWS):
                if k > 0 or h in FAR[1 - c]:
                    send(("p", k, h), psend.at[k, pl.ds(o, n)], pd.at[k, pl.ds(o, n)], sib)

        def touches(d, o, n):
            return o < SHARD if d == 0 else o + n > SHARD

        def own_rows(ref, pieces):
            mine = [(o, n) for o, n in pieces if touches(c, o, n)]
            lo, hi = mine[0][0], mine[-1][0] + mine[-1][1]
            return ref[lo:hi].astype(jnp.float32)[c * SHARD - lo:(c + 1) * SHARD - lo]

        def step_b(k, h):
            o, n = T_ROWS[h]
            slot = f_slot(k) if k else 7
            recv(("p", k, h), pd.at[k, pl.ds(o, n)])
            total = pbuf[slot * UNIT + o:slot * UNIT + o + n] + pd[k, o:o + n].astype(jnp.float32)
            more = {3: 0, 2: 3, 1: 2}.get(k)
            if k in (1, 2) or (k == 3 and h in FAR[c]):
                recv(("b", more, h), rr.at[k, pl.ds(o, n)])
                total = total + rr[k, o:o + n].astype(jnp.float32)
            rsb[k, o:o + n] = total.astype(jnp.bfloat16)
            if k == 1:
                for d in (0, 1):
                    if touches(d, o, n):
                        there = own_in.at[c, pl.ds(o, n)]
                        send(("e", c, h, d), rsb.at[k, pl.ds(o, n)], there, dev(x, y, z - 2 * sg, d))
            else:
                to = 3 if k == 0 else k - 1
                send(("b", k, h), rsb.at[k, pl.ds(o, n)], rr.at[to, pl.ds(o, n)], behind)

        def step_po():
            send("po", pbuf.at[pl.ds((1 - c) * SHARD, SHARD)], other, sib)

        def step_gt():
            recv("po", other)
            text_dir = pbuf[c * SHARD:(c + 1) * SHARD] + other[...]
            for way in (0, 1):
                for h, (o, n) in enumerate(T_ROWS):
                    if touches(c, o, n):
                        recv(("e", way, h, c), own_in.at[way, pl.ds(o, n)])
                text_dir = text_dir + own_rows(own_in.at[way], T_ROWS)
            v, v_inv = unit_rows(cap[...])
            grads[1] = (text_dir - v * jnp.sum(v * text_dir, axis=1, keepdims=True)) * v_inv

        def q_piece(slot, h):
            o, n = I_ROWS[h]
            return qbuf[slot * UNIT + o:slot * UNIT + o + n]

        def step_ro(a, h):
            n = LINE.index(a)
            o, m = I_ROWS[h]
            bsend[n, o:o + m] = q_piece(SLOT[a, 2], h).astype(jnp.bfloat16)
            here = pl.ds(o, m)
            send(("ro", a, h), bsend.at[n, here], rel_in.at[n, here], along_b(1 if a in RIGHT else -1))

        def step_rf(a, s, h):
            n = LINE.index(a)
            o, m = I_ROWS[h]
            here = pl.ds(o, m)
            total = q_piece(SLOT[a, s], h)
            if (a in RIGHT) == (s == 1):
                recv(("ro", a, h), rel_in.at[n, here])
                total = total + rel_in[n, o:o + m].astype(jnp.float32)
            to = n if s == 1 else 4 + n
            bsend[4 + to, o:o + m] = total.astype(jnp.bfloat16)
            send(("rf", a, s, h), bsend.at[4 + to, here], fin_in.at[to, here], along_b(s))

        def line_total(a, h):
            n = LINE.index(a)
            o, m = I_ROWS[h]
            here = pl.ds(o, m)
            recv(("rf", a, 1, h), fin_in.at[n, here])
            recv(("rf", a, -1, h), fin_in.at[4 + n, here])
            return (
                q_piece(SLOT[a, 0], h)
                + fin_in[n, o:o + m].astype(jnp.float32)
                + fin_in[4 + n, o:o + m].astype(jnp.float32)
            )

        def step_la(a, h):
            o, m = I_ROWS[h]
            here = pl.ds(o, m)
            total = line_total(a, h)
            i = {2: 0, 1: 1, -1: 2}[a]
            if (a == 1 and h in HALF[0]) or (a == -1 and h in HALF[1]):
                recv(("ra", h), half_in.at[here])
                total = total + half_in[o:o + m].astype(jnp.float32)
            asend[i, o:o + m] = total.astype(jnp.bfloat16)
            if a == 2:
                send(("ra", h), asend.at[i, here], half_in.at[here], along_a(1 if h in HALF[0] else -1))
            else:
                send(("rb", a, h), asend.at[i, here], afin_in.at[i - 1, here], along_a(a))

        def step_own(h):
            o, m = I_ROWS[h]
            here = pl.ds(o, m)
            total = line_total(0, h)
            for i, a in enumerate((1, -1)):
                recv(("rb", a, h), afin_in.at[i, here])
                total = total + afin_in[i, o:o + m].astype(jnp.float32)
            if c == 0:
                own_buf[o:o + m] = total
                if touches(1, o, m):
                    p = max(o, SHARD)
                    send(("s", h), own_buf.at[pl.ds(p, o + m - p)], sib_in.at[pl.ds(p - SHARD, o + m - p)], sib)
            else:
                last_send[o:o + m] = total.astype(jnp.bfloat16)
                for d in (0, 1):
                    if touches(d, o, m):
                        send(("l", h, d), last_send.at[here], last_in.at[here], dev(x, y, z - 1, d))

        def step_gi():
            if c == 0:
                mine = own_buf[0:SHARD]
            else:
                for h, (o, m) in enumerate(I_ROWS):
                    if touches(1, o, m):
                        p = max(o, SHARD)
                        recv(("s", h), sib_in.at[pl.ds(p - SHARD, o + m - p)])
                mine = sib_in[...]
            for h, (o, m) in enumerate(I_ROWS):
                if touches(c, o, m):
                    recv(("l", h, c), last_in.at[pl.ds(o, m)])
            image_dir = mine + own_rows(last_in, I_ROWS)
            u, u_inv = unit_rows(pic[...])
            grads[0] = (image_dir - u * jnp.sum(u * image_dir, axis=1, keepdims=True)) * u_inv

        steps = dict(
            t=step_t, i=step_i, W=step_w, P=step_p, Q=step_q, pp=step_pp, b=step_b, po=step_po, gt=step_gt,
            ro=step_ro, rf=step_rf, la=step_la, own=step_own, gi=step_gi,
        )
        for name, *args in ORDER[c]:
            steps[name](*args)
        for cp in started:
            cp.wait_send()

    for c in (0, 1):
        pl.when(core == c)(lambda c=c: one_core(c))


def body(picture_vectors, caption_vectors, scale_exponent, score_shift):
    bf16, f32 = jnp.bfloat16, jnp.float32
    vmem = pl.BlockSpec(memory_space=pltpu.VMEM)
    smem = pl.BlockSpec(memory_space=pltpu.SMEM)
    pairs = jnp.stack([picture_vectors, caption_vectors])
    grads = pl.pallas_call(
        kernel,
        out_shape=jax.ShapeDtypeStruct((2, SHARD, D), f32),
        in_specs=[vmem, smem, smem],
        out_specs=vmem,
        scratch_shapes=[
            pltpu.VMEM((SHARD, D), bf16),
            pltpu.VMEM((SHARD, D), bf16),
            pltpu.VMEM((SHARD, D), bf16),
            pltpu.VMEM((N_IMG, D), bf16),
            pltpu.VMEM((N_TXT, D), bf16),
            pltpu.VMEM((N_TXT, N_IMG), bf16),
            pltpu.VMEM((N_TXT, D), f32),
            pltpu.VMEM((N_IMG, D), f32),
            pltpu.VMEM((4, UNIT, D), bf16),
            pltpu.VMEM((4, UNIT, D), bf16),
            pltpu.VMEM((4, UNIT, D), bf16),
            pltpu.VMEM((4, UNIT, D), bf16),
            pltpu.VMEM((2, UNIT, D), bf16),
            pltpu.VMEM((SHARD, D), f32),
            pltpu.VMEM((4, UNIT, D), bf16),
            pltpu.VMEM((8, UNIT, D), bf16),
            pltpu.VMEM((UNIT, D), bf16),
            pltpu.VMEM((2, UNIT, D), bf16),
            pltpu.VMEM((12, UNIT, D), bf16),
            pltpu.VMEM((3, UNIT, D), bf16),
            pltpu.VMEM((UNIT, D), bf16),
            pltpu.VMEM((UNIT, D), bf16),
            pltpu.VMEM((UNIT, D), f32),
            pltpu.VMEM((SHARD, D), f32),
            pltpu.SemaphoreType.DMA((192,)),
            pltpu.SemaphoreType.DMA((192,)),
        ],
        compiler_params=pltpu.CompilerParams(
            collective_id=0, has_side_effects=True, vmem_limit_bytes=34 * 2**20
        ),
    )(pairs, scale_exponent, score_shift)
    return grads[0], grads[1]


def solution(mesh):
    return jax.shard_map(
        body,
        mesh=mesh,
        in_specs=(P(("row", "col"), None), P(("col", "row"), None), P(), P()),
        out_specs=(P(("row", "col"), None), P(("col", "row"), None)),
        check_vma=False,
    )
```

```python
import jax
import jax.numpy as jnp
from jax import lax
from jax.experimental import pallas as pl
from jax.experimental.pallas import tpu as pltpu
from jax.sharding import PartitionSpec as P

MESH = pl.DeviceIdType.MESH
D = 1152
SHARD = 40
UNIT = 80
SLOTS = (
    (0, 0), (1, 0), (-1, 0), (2, 0), (0, 1), (0, -1), (1, 1), (1, -1),
    (-1, 1), (-1, -1), (2, 1), (2, -1), (0, 2), (1, 2), (-1, 2), (2, 2),
)
SLOT = {ab: i for i, ab in enumerate(SLOTS)}
RIGHT = (0, 2)
LINE = (0, 1, -1, 2)
N_IMG = 16 * UNIT
N_TXT = 8 * UNIT
T_ROWS = ((0, 32), (32, 16), (48, 32))
I_ROWS = ((0, 32), (32, 16), (48, 32))
HALF = ((0, 1), (2,))
FAR = ((1,), (0, 2))
ROUTE = ({}, {})
DIRECT = ()
W_BLOCKS = ((0, 240, 0, 640), (240, 400, 0, 640), (0, 400, 640, 1024), (400, 640, 0, 1024), (0, 640, 1024, 1280))
P_GROUPS = ((400, 640, 0, 1280), (240, 400, 0, 1280), (0, 240, 0, 1280))
Q_GROUPS = ((896, 1280), (256, 896), (0, 256))
ORDER = (
    (
        ('t', 0, 1), ('i', 0, 0), ('i', 0, 1), ('i', 0, 2), ('t', 0, 0), ('t', 0, 2), ('i', 4, 0), ('i', 5, 0),
        ('i', 2, 0), ('i', 1, 0), ('i', 2, 1), ('t', 1, 1), ('i', 5, 1), ('i', 1, 1), ('i', 4, 1), ('i', 1, 2),
        ('i', 2, 2), ('i', 4, 2), ('i', 5, 2), ('t', 1, 0), ('t', 1, 2), ('i', 12, 0), ('i', 8, 0), ('i', 3, 0),
        ('t', 2, 1), ('i', 3, 1), ('i', 3, 2), ('i', 9, 0), ('i', 6, 0), ('i', 8, 1), ('i', 6, 1), ('t', 2, 0),
        ('i', 7, 0), ('i', 6, 2), ('i', 9, 1), ('i', 8, 2), ('t', 2, 2), ('i', 12, 1), ('i', 7, 1), ('t', 3, 1),
        ('i', 7, 2), ('i', 14, 0), ('W', 0), ('i', 9, 2), ('i', 10, 0), ('W', 1), ('t', 3, 0), ('i', 10, 1),
        ('i', 12, 2), ('i', 10, 2), ('i', 11, 0), ('i', 11, 1), ('i', 13, 0), ('i', 14, 1), ('t', 3, 2),
        ('i', 13, 1), ('i', 11, 2), ('W', 2), ('t', 4, 1), ('i', 13, 2), ('i', 14, 2), ('i', 15, 0), ('i', 15, 1),
        ('i', 15, 2), ('W', 4), ('W', 3), ('P', 0), ('pp', 0), ('pp', 3), ('b', 0, 1), ('b', 3, 0), ('b', 3, 2),
        ('Q', 0), ('ro', -1, 2), ('ro', 2, 1), ('ro', 2, 0), ('ro', -1, 1), ('ro', -1, 0), ('ro', 2, 2),
        ('ro', 1, 2), ('ro', 1, 0), ('ro', 0, 2), ('ro', 0, 1), ('ro', 1, 1), ('ro', 0, 0), ('P', 1), ('pp', 2),
        ('Q', 1), ('rf', 2, -1, 1), ('rf', 2, -1, 2), ('rf', 1, 1, 1), ('rf', 2, -1, 0), ('b', 3, 1),
        ('rf', 1, 1, 2), ('b', 2, 0), ('rf', 2, 1, 1), ('rf', 2, 1, 0), ('rf', -1, -1, 0), ('rf', 2, 1, 2),
        ('rf', -1, -1, 2), ('rf', 0, -1, 2), ('rf', -1, 1, 2), ('rf', -1, 1, 0), ('rf', 0, -1, 0), ('rf', 1, 1, 0),
        ('rf', 1, -1, 2), ('rf', 0, 1, 2), ('rf', -1, 1, 1), ('rf', -1, -1, 1), ('rf', 0, -1, 1), ('Q', 2),
        ('rf', 1, -1, 1), ('b', 2, 2), ('rf', 1, -1, 0), ('rf', 0, 1, 1), ('rf', 0, 1, 0), ('P', 2), ('pp', 1),
        ('po',), ('la', 2, 1), ('b', 2, 1), ('la', 2, 0), ('b', 1, 0), ('la', 2, 2), ('b', 1, 2), ('b', 1, 1),
        ('la', -1, 0), ('la', -1, 2), ('la', 1, 2), ('la', -1, 1), ('la', 1, 1), ('la', 1, 0), ('own', 2), ('gt',),
        ('own', 1), ('own', 0), ('gi',),
    ),
    (
        ('t', 0, 0), ('t', 0, 2), ('t', 0, 1), ('i', 0, 0), ('i', 0, 1), ('i', 0, 2), ('t', 1, 0), ('t', 1, 2),
        ('i', 1, 0), ('i', 4, 0), ('i', 5, 0), ('i', 2, 0), ('t', 1, 1), ('i', 4, 1), ('i', 1, 1), ('i', 5, 1),
        ('i', 2, 1), ('i', 4, 2), ('i', 1, 2), ('i', 5, 2), ('i', 2, 2), ('t', 2, 0), ('i', 7, 0), ('i', 6, 0),
        ('i', 12, 0), ('i', 8, 0), ('i', 3, 0), ('t', 2, 2), ('i', 6, 1), ('i', 8, 1), ('i', 9, 0), ('i', 3, 1),
        ('t', 2, 1), ('i', 7, 1), ('i', 12, 1), ('i', 6, 2), ('i', 9, 1), ('i', 3, 2), ('i', 8, 2), ('i', 7, 2),
        ('W', 1), ('t', 3, 0), ('i', 13, 0), ('i', 12, 2), ('W', 0), ('i', 14, 0), ('i', 9, 2), ('i', 10, 0),
        ('t', 3, 2), ('i', 11, 0), ('i', 13, 1), ('i', 11, 1), ('i', 14, 1), ('t', 3, 1), ('i', 10, 1), ('i', 11, 2),
        ('i', 13, 2), ('i', 10, 2), ('W', 2), ('t', 4, 0), ('i', 14, 2), ('i', 15, 0), ('i', 15, 1), ('i', 15, 2),
        ('t', 4, 2), ('W', 3), ('W', 4), ('P', 0), ('pp', 3), ('pp', 0), ('Q', 0), ('ro', -1, 0), ('ro', 2, 0),
        ('ro', 2, 2), ('ro', 1, 0), ('ro', -1, 1), ('ro', 1, 2), ('ro', -1, 2), ('ro', 1, 1), ('ro', 2, 1),
        ('ro', 0, 2), ('ro', 0, 0), ('b', 0, 0), ('ro', 0, 1), ('b', 0, 2), ('P', 1), ('b', 3, 1), ('pp', 2),
        ('Q', 1), ('rf', 2, -1, 1), ('rf', 2, 1, 0), ('rf', 2, -1, 0), ('rf', -1, 1, 2), ('rf', 1, 1, 1),
        ('rf', 2, 1, 2), ('rf', -1, -1, 1), ('rf', 2, 1, 1), ('rf', 2, -1, 2), ('rf', -1, 1, 1), ('rf', -1, -1, 0),
        ('rf', 1, 1, 2), ('rf', 0, -1, 1), ('rf', 1, -1, 0), ('rf', -1, 1, 0), ('rf', 1, 1, 0), ('rf', 0, -1, 2),
        ('rf', 0, -1, 0), ('rf', 1, -1, 2), ('b', 3, 0), ('rf', 0, 1, 2), ('P', 2), ('pp', 1), ('b', 3, 2),
        ('rf', -1, -1, 2), ('rf', 1, -1, 1), ('rf', 0, 1, 1), ('po',), ('rf', 0, 1, 0), ('Q', 2), ('la', 2, 0),
        ('b', 2, 1), ('la', 2, 2), ('la', 2, 1), ('la', -1, 1), ('b', 2, 0), ('la', -1, 0), ('b', 2, 2),
        ('la', 1, 0), ('b', 1, 1), ('la', 1, 2), ('la', -1, 2), ('la', 1, 1), ('b', 1, 0), ('own', 0), ('b', 1, 2),
        ('own', 2), ('own', 1), ('gt',), ('gi',),
    ),
)


def unit_rows(values):
    values = values.astype(jnp.float32)
    inverse = lax.rsqrt(jnp.sum(values * values, axis=1, keepdims=True) + 1e-06)
    return values * inverse, inverse


def kernel(
    raw, scale, shift, grads,
    raw_cap, raw_a, raw_b, img, txt, wt, pbuf, qbuf,
    psend, pd, rsb, rr, own_in, other,
    rel_in, fin_in, half_in, afin_in, bsend, asend, last_send, last_in, own_buf, sib_in,
    ssem, rsem,
):
    r = lax.axis_index("row")
    q = lax.axis_index("col")
    x, y, z, core = (q % 8) // 2, r // 8, (q // 8) * 8 + r % 8, q % 2

    def dev(x, y, z, c):
        x, y, z = (x + 4) % 4, (y + 4) % 4, (z + 16) % 16
        return (y * 8 + z % 8, (z // 8) * 8 + x * 2 + c)

    barrier = pltpu.get_barrier_semaphore()

    def greet(to):
        pl.semaphore_signal(barrier, inc=1, device_id=to, device_id_type=MESH)

    for to in (
        dev(x, y, z, 1 - core), dev(x + 1, y, z, core), dev(x - 1, y, z, core), dev(x, y + 1, z, core),
        dev(x, y - 1, z, core), dev(x, y, z + 2, core), dev(x, y, z - 2, core), dev(x, y, z + 1, 1),
        dev(x, y, z - 2 + 4 * core, 1 - core),
    ):
        greet(to)

    @pl.when(core == 1)
    def _():
        greet(dev(x, y, z - 1, 1))
        greet(dev(x, y, z - 1, 0))

    for c in DIRECT:
        @pl.when(core == c)
        def _(c=c):
            greet(dev(x + 2 * (1 - c), y + 2 * c, z, c))

    pic, cap = raw.at[0], raw.at[1]
    ids = {}
    offset = shift[0]

    def one_core(c):
        sib = dev(x, y, z, 1 - c)
        sg = 1 - 2 * c
        ahead = dev(x, y, z + 2 * sg, c)
        behind = dev(x, y, z - 2 * sg, c)
        started = []

        def along_a(s):
            return dev(x + s * (1 - c), y + s * c, z, c)

        def along_b(s):
            return dev(x + s * c, y + s * (1 - c), z, c)

        def rcopy(key, src, dst, to):
            i = ids.setdefault(key, len(ids))
            return pltpu.make_async_remote_copy(
                src_ref=src, dst_ref=dst, send_sem=ssem.at[i], recv_sem=rsem.at[i],
                device_id=to, device_id_type=MESH,
            )

        def send(key, src, dst, to):
            cp = rcopy(key, src, dst, to)
            cp.start()
            started.append(cp)

        def recv(key, dst):
            rcopy(key, dst, dst, sib).wait_recv()

        smooth = jnp.exp(jnp.full((1, 128), scale[0], jnp.float32))[:, :1]
        lane = lax.broadcasted_iota(jnp.int32, (1, N_IMG), 1)
        zi = (z - c + 16) % 16
        img_ids = lane
        before = None
        for s, (a, b) in enumerate(SLOTS):
            xs = (x + a * (1 - c) + b * c + 4) % 4
            ys = (y + a * c + b * (1 - c) + 4) % 4
            base = ((ys * 8 + zi % 8) * 16 + (zi // 8) * 8 + xs * 2) * SHARD
            if s == 0:
                img_ids = img_ids + base
            else:
                img_ids = img_ids + jnp.where(lane >= s * UNIT, base - before - UNIT, 0)
            before = base
        row_in = lax.broadcasted_iota(jnp.int32, (UNIT, 1), 0)
        row_in = row_in + jnp.where(row_in >= SHARD, 32 * SHARD - SHARD, 0)

        def txt_ids(slot):
            step = 0 if slot == 0 else (8 if slot == 7 else (-2 * ((slot + 1) // 2) if slot % 2 else slot))
            zt = (z + step + 16) % 16
            return row_in + (((zt // 8) * 8 + x * 2) * 32 + y * 8 + zt % 8) * SHARD

        pl.semaphore_wait(barrier, (11 if c else 9) + (1 if c in DIRECT else 0))
        send("cap", cap, raw_cap, sib)
        if c == 0:
            send("pic_a", pic, raw_a, dev(x, y, z + 1, 1))
        else:
            send("pic_0", pic, raw_a, sib)
            send("pic_b", pic, raw_b, dev(x, y, z + 1, 1))
        own_txt = unit_rows(cap[...])[0]
        if c == 0:
            own_img = unit_rows(pic[...])[0]

        def both(one, two):
            return jnp.concatenate([one, two], axis=0).astype(jnp.bfloat16)

        def f_slot(k):
            return 0 if k == 0 else (7 if k == 4 else 2 * k - 1 + c)

        def g_slot(k):
            return 7 if k == 4 else 2 * k - c

        def t_piece(slot, h):
            return pl.ds(slot * UNIT + T_ROWS[h][0], T_ROWS[h][1])

        def i_piece(slot, h):
            return pl.ds(slot * UNIT + I_ROWS[h][0], I_ROWS[h][1])

        got = set()

        def need(key, dst):
            if key not in got:
                got.add(key)
                recv(key, dst)

        def step_t(k, h):
            if k == 0:
                if "txt" not in got:
                    got.add("txt")
                    recv("cap", raw_cap)
                    other = unit_rows(raw_cap[...])[0]
                    txt[0:UNIT] = both(own_txt, other) if c == 0 else both(other, own_txt)
            else:
                need(("t", k, h), txt.at[t_piece(f_slot(k), h)])
            here = txt.at[t_piece(f_slot(k), h)]
            if k < 3 or (k == 3 and h in FAR[c]):
                send(("t", k + 1, h), here, txt.at[t_piece(f_slot(k + 1), h)], ahead)
            if k > 0:
                send(("g", k, h), here, here, sib)

        def step_i(s, h):
            a, b = SLOTS[s]

            def forward(to_slot, to):
                send(("i", to_slot, h), img.at[i_piece(s, h)], img.at[i_piece(to_slot, h)], to)

            if s == 0:
                if "img" not in got:
                    got.add("img")
                    if c == 0:
                        recv("pic_0", raw_a)
                        img[0:UNIT] = both(own_img, unit_rows(raw_a[...])[0])
                    else:
                        recv("pic_a", raw_a)
                        recv("pic_b", raw_b)
                        img[0:UNIT] = both(unit_rows(raw_a[...])[0], unit_rows(raw_b[...])[0])
                forward(SLOT[-1, 0], along_a(1))
                forward(SLOT[1, 0], along_a(-1))
            else:
                need(("i", s, h), img.at[i_piece(s, h)])
            if b == 0:
                if a == -1 and h in HALF[0] and c not in DIRECT:
                    forward(SLOT[2, 0], along_a(1))
                if a == 1 and h in HALF[1] and c not in DIRECT:
                    forward(SLOT[2, 0], along_a(-1))
                forward(SLOT[a, -1], along_b(1))
                forward(SLOT[a, 1], along_b(-1))
                if a == 0 and c in DIRECT:
                    forward(SLOT[2, 0], along_a(2))

            def way(a):
                return ROUTE[c].get((a, h), (0, 1) if a in RIGHT else (0, -1))

            if abs(b) == 1 and way(a) == (0, -b):
                forward(SLOT[a, 2], along_b(-b))
            if (a, b) == (0, 2):
                for s_a in (-1, 1):
                    if way(s_a) == (-s_a, 0):
                        forward(SLOT[s_a, 2], along_a(-s_a))

        def text_needs(slot):
            if slot == 0:
                return
            k = 4 if slot == 7 else (slot + 1) // 2
            for h in range(len(T_ROWS)):
                mine = h in FAR[c] if k == 4 else (slot % 2 == 1) == (c == 0)
                if not mine:
                    need(("g", k, h), txt.at[t_piece(slot, h)])

        def step_w(n):
            t0, t1, i0, i1 = W_BLOCKS[n]
            for s in range(t0 // UNIT, t1 // UNIT):
                text_needs(s)
            dots = lax.dot_general(
                txt[t0:t1], img[i0:i1], (((1,), (1,)), ((), ())), preferred_element_type=jnp.float32
            )
            logits = smooth * dots + offset
            tid = jnp.concatenate([txt_ids(s) for s in range(t0 // UNIT, t1 // UNIT)], axis=0)
            match = tid == img_ids[:, i0:i1]
            value = smooth / (1.0 + jnp.exp(jnp.where(match, logits, -logits)))
            wt[t0:t1, i0:i1] = jnp.where(match, -value, value).astype(jnp.bfloat16)

        def step_p(g):
            t0, t1, k0, k1 = P_GROUPS[g]
            part = jnp.dot(wt[t0:t1, k0:k1], img[k0:k1], preferred_element_type=jnp.float32)
            pbuf[t0:t1] = part if k0 == 0 else pbuf[t0:t1] + part

        def step_q(g):
            i0, i1 = Q_GROUPS[g]
            qbuf[i0:i1] = lax.dot_general(
                wt[:, i0:i1], txt[...], (((0,), (0,)), ((), ())), preferred_element_type=jnp.float32
            )

        def step_pp(k):
            slot = g_slot(k) if k else 7
            psend[k] = pbuf[slot * UNIT:(slot + 1) * UNIT].astype(jnp.bfloat16)
            for h, (o, n) in enumerate(T_ROWS):
                if k > 0 or h in FAR[1 - c]:
                    send(("p", k, h), psend.at[k, pl.ds(o, n)], pd.at[k, pl.ds(o, n)], sib)

        def touches(d, o, n):
            return o < SHARD if d == 0 else o + n > SHARD

        def own_rows(ref, pieces):
            mine = [(o, n) for o, n in pieces if touches(c, o, n)]
            lo, hi = mine[0][0], mine[-1][0] + mine[-1][1]
            return ref[lo:hi].astype(jnp.float32)[c * SHARD - lo:(c + 1) * SHARD - lo]

        def step_b(k, h):
            o, n = T_ROWS[h]
            slot = f_slot(k) if k else 7
            recv(("p", k, h), pd.at[k, pl.ds(o, n)])
            total = pbuf[slot * UNIT + o:slot * UNIT + o + n] + pd[k, o:o + n].astype(jnp.float32)
            more = {3: 0, 2: 3, 1: 2}.get(k)
            if k in (1, 2) or (k == 3 and h in FAR[c]):
                recv(("b", more, h), rr.at[k, pl.ds(o, n)])
                total = total + rr[k, o:o + n].astype(jnp.float32)
            rsb[k, o:o + n] = total.astype(jnp.bfloat16)
            if k == 1:
                for d in (0, 1):
                    if touches(d, o, n):
                        there = own_in.at[c, pl.ds(o, n)]
                        send(("e", c, h, d), rsb.at[k, pl.ds(o, n)], there, dev(x, y, z - 2 * sg, d))
            else:
                to = 3 if k == 0 else k - 1
                send(("b", k, h), rsb.at[k, pl.ds(o, n)], rr.at[to, pl.ds(o, n)], behind)

        def step_po():
            send("po", pbuf.at[pl.ds((1 - c) * SHARD, SHARD)], other, sib)

        def step_gt():
            recv("po", other)
            text_dir = pbuf[c * SHARD:(c + 1) * SHARD] + other[...]
            for way in (0, 1):
                for h, (o, n) in enumerate(T_ROWS):
                    if touches(c, o, n):
                        recv(("e", way, h, c), own_in.at[way, pl.ds(o, n)])
                text_dir = text_dir + own_rows(own_in.at[way], T_ROWS)
            v, v_inv = unit_rows(cap[...])
            grads[1] = (text_dir - v * jnp.sum(v * text_dir, axis=1, keepdims=True)) * v_inv

        def q_piece(slot, h):
            o, n = I_ROWS[h]
            return qbuf[slot * UNIT + o:slot * UNIT + o + n]

        def step_ro(a, h):
            n = LINE.index(a)
            o, m = I_ROWS[h]
            bsend[n, o:o + m] = q_piece(SLOT[a, 2], h).astype(jnp.bfloat16)
            here = pl.ds(o, m)
            send(("ro", a, h), bsend.at[n, here], rel_in.at[n, here], along_b(1 if a in RIGHT else -1))

        def step_rf(a, s, h):
            n = LINE.index(a)
            o, m = I_ROWS[h]
            here = pl.ds(o, m)
            total = q_piece(SLOT[a, s], h)
            if (a in RIGHT) == (s == 1):
                recv(("ro", a, h), rel_in.at[n, here])
                total = total + rel_in[n, o:o + m].astype(jnp.float32)
            to = n if s == 1 else 4 + n
            bsend[4 + to, o:o + m] = total.astype(jnp.bfloat16)
            send(("rf", a, s, h), bsend.at[4 + to, here], fin_in.at[to, here], along_b(s))

        def line_total(a, h):
            n = LINE.index(a)
            o, m = I_ROWS[h]
            here = pl.ds(o, m)
            recv(("rf", a, 1, h), fin_in.at[n, here])
            recv(("rf", a, -1, h), fin_in.at[4 + n, here])
            return (
                q_piece(SLOT[a, 0], h)
                + fin_in[n, o:o + m].astype(jnp.float32)
                + fin_in[4 + n, o:o + m].astype(jnp.float32)
            )

        def step_la(a, h):
            o, m = I_ROWS[h]
            here = pl.ds(o, m)
            total = line_total(a, h)
            i = {2: 0, 1: 1, -1: 2}[a]
            if (a == 1 and h in HALF[0]) or (a == -1 and h in HALF[1]):
                recv(("ra", h), half_in.at[here])
                total = total + half_in[o:o + m].astype(jnp.float32)
            asend[i, o:o + m] = total.astype(jnp.bfloat16)
            if a == 2:
                send(("ra", h), asend.at[i, here], half_in.at[here], along_a(1 if h in HALF[0] else -1))
            else:
                send(("rb", a, h), asend.at[i, here], afin_in.at[i - 1, here], along_a(a))

        def step_own(h):
            o, m = I_ROWS[h]
            here = pl.ds(o, m)
            total = line_total(0, h)
            for i, a in enumerate((1, -1)):
                recv(("rb", a, h), afin_in.at[i, here])
                total = total + afin_in[i, o:o + m].astype(jnp.float32)
            if c == 0:
                own_buf[o:o + m] = total
                if touches(1, o, m):
                    p = max(o, SHARD)
                    send(("s", h), own_buf.at[pl.ds(p, o + m - p)], sib_in.at[pl.ds(p - SHARD, o + m - p)], sib)
            else:
                last_send[o:o + m] = total.astype(jnp.bfloat16)
                for d in (0, 1):
                    if touches(d, o, m):
                        send(("l", h, d), last_send.at[here], last_in.at[here], dev(x, y, z - 1, d))

        def step_gi():
            if c == 0:
                mine = own_buf[0:SHARD]
            else:
                for h, (o, m) in enumerate(I_ROWS):
                    if touches(1, o, m):
                        p = max(o, SHARD)
                        recv(("s", h), sib_in.at[pl.ds(p - SHARD, o + m - p)])
                mine = sib_in[...]
            for h, (o, m) in enumerate(I_ROWS):
                if touches(c, o, m):
                    recv(("l", h, c), last_in.at[pl.ds(o, m)])
            image_dir = mine + own_rows(last_in, I_ROWS)
            u, u_inv = unit_rows(pic[...])
            grads[0] = (image_dir - u * jnp.sum(u * image_dir, axis=1, keepdims=True)) * u_inv

        steps = dict(
            t=step_t, i=step_i, W=step_w, P=step_p, Q=step_q, pp=step_pp, b=step_b, po=step_po, gt=step_gt,
            ro=step_ro, rf=step_rf, la=step_la, own=step_own, gi=step_gi,
        )
        for name, *args in ORDER[c]:
            steps[name](*args)
        for cp in started:
            cp.wait_send()

    for c in (0, 1):
        pl.when(core == c)(lambda c=c: one_core(c))


def body(picture_vectors, caption_vectors, scale_exponent, score_shift):
    bf16, f32 = jnp.bfloat16, jnp.float32
    vmem = pl.BlockSpec(memory_space=pltpu.VMEM)
    smem = pl.BlockSpec(memory_space=pltpu.SMEM)
    pairs = jnp.stack([picture_vectors, caption_vectors])
    grads = pl.pallas_call(
        kernel,
        out_shape=jax.ShapeDtypeStruct((2, SHARD, D), f32),
        in_specs=[vmem, smem, smem],
        out_specs=vmem,
        scratch_shapes=[
            pltpu.VMEM((SHARD, D), bf16),
            pltpu.VMEM((SHARD, D), bf16),
            pltpu.VMEM((SHARD, D), bf16),
            pltpu.VMEM((N_IMG, D), bf16),
            pltpu.VMEM((N_TXT, D), bf16),
            pltpu.VMEM((N_TXT, N_IMG), bf16),
            pltpu.VMEM((N_TXT, D), f32),
            pltpu.VMEM((N_IMG, D), f32),
            pltpu.VMEM((4, UNIT, D), bf16),
            pltpu.VMEM((4, UNIT, D), bf16),
            pltpu.VMEM((4, UNIT, D), bf16),
            pltpu.VMEM((4, UNIT, D), bf16),
            pltpu.VMEM((2, UNIT, D), bf16),
            pltpu.VMEM((SHARD, D), f32),
            pltpu.VMEM((4, UNIT, D), bf16),
            pltpu.VMEM((8, UNIT, D), bf16),
            pltpu.VMEM((UNIT, D), bf16),
            pltpu.VMEM((2, UNIT, D), bf16),
            pltpu.VMEM((12, UNIT, D), bf16),
            pltpu.VMEM((3, UNIT, D), bf16),
            pltpu.VMEM((UNIT, D), bf16),
            pltpu.VMEM((UNIT, D), bf16),
            pltpu.VMEM((UNIT, D), f32),
            pltpu.VMEM((SHARD, D), f32),
            pltpu.SemaphoreType.DMA((192,)),
            pltpu.SemaphoreType.DMA((192,)),
        ],
        compiler_params=pltpu.CompilerParams(
            collective_id=0, has_side_effects=True, vmem_limit_bytes=34 * 2**20
        ),
    )(pairs, scale_exponent, score_shift)
    return grads[0], grads[1]


def solution(mesh):
    return jax.shard_map(
        body,
        mesh=mesh,
        in_specs=(P(("row", "col"), None), P(("col", "row"), None), P(), P()),
        out_specs=(P(("row", "col"), None), P(("col", "row"), None)),
        check_vma=False,
    )
```
